128 devices in a mesh: fsdp: 16 (over y_hi, x, core), tp: 8 (over y_lo, z).
Axes of the slice: x: 4, y: 4 (y_hi: 2, y_lo: 2; y = y_hi * 2 + y_lo), z: 4, core: 2. Of those that a mesh axis runs over, the one named last changes fastest.
Arguments:
- hidden_in: bfloat16 [8192, 4096], P('fsdp'), may hold values from -6 to 6
- w_gate: bfloat16 [4096, 8192], P(('fsdp', 'tp')), may hold values from -0.09375 to 0.09375
- w_input: bfloat16 [4096, 8192], P(('fsdp', 'tp')), may hold values from -0.09375 to 0.09375
- w_groups: bfloat16 [4096, 4096], P(('fsdp', 'tp')), may hold values from -0.09375 to 0.09375
- w_step: bfloat16 [4096, 128], P(('fsdp', 'tp')), may hold values from -0.09375 to 0.09375
- w_out: bfloat16 [8192, 4096], P('tp', 'fsdp'), may hold values from -0.0625 to 0.0625
- conv_input: bfloat16 [4, 8192], P(None, 'tp'), may hold values from -3 to 3
- conv_groups: bfloat16 [4, 4096], P(None, 'tp'), may hold values from -3 to 3
- tail_input: bfloat16 [64, 3, 8192], P('fsdp', None, 'tp'), may hold values from -6 to 6
- tail_groups: bfloat16 [64, 3, 4096], P('fsdp', None, 'tp'), may hold values from -6 to 6
- init_state: float32 [64, 128, 64, 256], P('fsdp', 'tp'), may hold values from -2.4 to 2.4
- a_rate: float32 [128], P('tp'), as said below
- step_bias: float32 [128], P('tp'), may hold values from -3.5 to -2.5
- skip_gain: float32 [128], P('tp'), may hold values from 0.5 to 1.5
- norm_gain: float32 [8192], P('tp'), may hold values from 0.1 to 1.9
- offsets: int32 [64], P('fsdp'), may hold values from 1 to 128, as said below
Outputs:
- mixed: bfloat16 [8192, 4096], P(('fsdp', 'tp'))
- final_state: float32 [64, 128, 64, 256], P('fsdp', 'tp')
The draws below stay inside these ranges and needn't reach their ends.
Inputs may be any that keep to these rules, and one draw needn't show every extreme that they name: `a_rate`: rates of the heads' decay; positive. `offsets`: every offset lies in 1 to 128; some rollout has all 128 tokens live in every draw.
All inputs are finite; a program needn't handle non-finite values.
Results may differ from the reference program's by a relative error of at most 0.024.
Values may be sent and summed in bfloat16 or wider, within the bound.
No kernel may reach another device: no remote copies, remote signals or barrier semaphores. Data moves between devices by JAX's collectives and lax.ppermute only.
A program may use at most 128 MiB of HBM per device.

```python
import jax
import jax.numpy as jnp
from jax import lax

D = 4096
H = 128
P_SIZE = 64
N = 256
G = 8
CONV = 4
LEN = 128
ROLLOUTS = 64
TOKENS = 8192
N_TP = 8


def draw_a_rate(key, part):
    key = jax.random.fold_in(key, 11)
    first, second, third = jax.random.split(key, 3)
    share = 0.5
    quick = jax.random.uniform(first, (H,), jnp.float32) < share
    slow_rate = jnp.exp(jax.random.uniform(second, (H,), jnp.float32, jnp.log(0.15), jnp.log(0.6)))
    fast_rate = jnp.exp(jax.random.uniform(third, (H,), jnp.float32, jnp.log(2.0), jnp.log(6.0)))
    return jnp.where(quick, fast_rate, slow_rate).astype(jnp.float32)


def draw_offsets(key, part):
    key = jax.random.fold_in(key, 23)
    first, second = jax.random.split(key, 2)
    drawn = jax.random.randint(first, (ROLLOUTS,), 1, LEN + 1, dtype=jnp.int32)
    filled = jax.random.randint(second, (), 0, ROLLOUTS, dtype=jnp.int32)
    return drawn.at[filled].set(LEN).astype(jnp.int32)


def shard_levels(key, dims, shards, smallest, high):
    factor_of = 1.0
    for axis_at, shards_of in shards:
        draws = jax.random.uniform(jax.random.fold_in(jax.random.fold_in(key, 6), axis_at), (shards_of,), jnp.float32, smallest / len(shards), high / len(shards))
        factor_of = factor_of * jnp.repeat(jnp.exp(draws), dims[axis_at] // shards_of).reshape((-1,) + (1,) * (len(dims) - 1 - axis_at))
    return factor_of


def scatter_about(own_key, shape, spread, reach, shards=(), kind=jnp.bfloat16):
    array = jax.random.normal(own_key, shape, jnp.float32) * spread
    if len(shards) > 0:
        array = shard_levels(own_key, shape, shards, -0.22, 0.18) * array
    return jnp.clip(array, min=-reach, max=reach).astype(kind)


def setup_inputs(seed: int = 0) -> dict:
    keys = jax.random.split(jax.random.key(seed), 17)
    return {
        "hidden_in": scatter_about(keys[0], (TOKENS, D), 1.0, 6.0, ((0, 16),)),
        "w_gate": scatter_about(keys[1], (D, H * P_SIZE), D ** -0.5, 0.09375, ((0, 128),)),
        "w_input": scatter_about(keys[2], (D, H * P_SIZE), D ** -0.5, 0.09375, ((0, 128),)),
        "w_groups": scatter_about(keys[3], (D, 2 * G * N), D ** -0.5, 0.09375, ((0, 128),)),
        "w_step": scatter_about(keys[4], (D, H), D ** -0.5, 0.09375, ((0, 128),)),
        "w_out": scatter_about(keys[5], (H * P_SIZE, D), (H * P_SIZE) ** -0.5, 0.0625, ((0, 8), (1, 16))),
        "conv_input": scatter_about(keys[6], (CONV, H * P_SIZE), CONV ** -0.5, 3.0, ((1, 8),)),
        "conv_groups": scatter_about(keys[7], (CONV, 2 * G * N), CONV ** -0.5, 3.0, ((1, 8),)),
        "tail_input": scatter_about(keys[8], (ROLLOUTS, CONV - 1, H * P_SIZE), 1.0, 6.0, ((0, 16), (2, 8))),
        "tail_groups": scatter_about(keys[9], (ROLLOUTS, CONV - 1, 2 * G * N), 1.0, 6.0, ((0, 16), (2, 8))),
        "init_state": scatter_about(keys[10], (ROLLOUTS, H, P_SIZE, N), 0.3, 2.4, ((0, 16), (1, 8)), jnp.float32),
        "a_rate": draw_a_rate(jax.random.fold_in(keys[16], 71), 0),
        "step_bias": jnp.clip(-3.5 + 1.0 * jax.random.uniform(keys[12], (H,), jnp.float32) ** shard_levels(keys[12], (H,), ((0, 8),), -0.2, 0.2), -3.5, -2.5),
        "skip_gain": jnp.clip(0.5 + 1.0 * jax.random.uniform(keys[13], (H,), jnp.float32) ** shard_levels(keys[13], (H,), ((0, 8),), -0.2, 0.2), 0.5, 1.5),
        "norm_gain": jnp.clip(1.0 + 0.18 * jax.random.normal(keys[14], (H * P_SIZE,), jnp.float32), 0.1, 1.9),
        "offsets": draw_offsets(jax.random.fold_in(keys[16], 71), 0),
    }


def convolve(tail, sequence, taps):
    padded = jnp.concatenate([tail, sequence], axis=1).astype(jnp.float32)
    weights = taps.astype(jnp.float32)
    length = sequence.shape[1]
    summed = jnp.zeros(sequence.shape, jnp.float32)
    for offset in range(CONV):
        summed = summed + weights[offset][None, None, :] * padded[:, offset:offset + length]
    return jax.nn.silu(summed)

def reference(hidden_in, w_gate, w_input, w_groups, w_step, w_out, conv_input, conv_groups, tail_input, tail_groups, init_state, a_rate, step_bias, skip_gain, norm_gain, offsets):
    gate_z = jnp.dot(hidden_in, w_gate, preferred_element_type=jnp.float32).astype(jnp.bfloat16)
    x_raw = jnp.dot(hidden_in, w_input, preferred_element_type=jnp.float32).astype(jnp.bfloat16)
    bc_raw = jnp.dot(hidden_in, w_groups, preferred_element_type=jnp.float32).astype(jnp.bfloat16)
    step_raw = jnp.dot(hidden_in, w_step, preferred_element_type=jnp.float32).astype(jnp.bfloat16)
    x_conv = convolve(tail_input, x_raw.reshape(ROLLOUTS, LEN, H * P_SIZE), conv_input)
    bc_conv = convolve(tail_groups, bc_raw.reshape(ROLLOUTS, LEN, 2 * G * N), conv_groups)
    x_heads = x_conv.reshape(ROLLOUTS, LEN, H, P_SIZE)
    grouped = bc_conv.reshape(ROLLOUTS, LEN, G, 2, N)
    b_heads = jnp.repeat(grouped[:, :, :, 0], H // G, axis=2)
    c_heads = jnp.repeat(grouped[:, :, :, 1], H // G, axis=2)
    live = (jnp.arange(LEN)[None, :] < offsets[:, None]).astype(jnp.float32)
    step = jax.nn.softplus(step_raw.reshape(ROLLOUTS, LEN, H).astype(jnp.float32) + step_bias[None, None, :]) * live[:, :, None]
    decay = jnp.exp(-a_rate[None, None, :] * step)

    def advance(state, inputs):
        x_now, b_now, c_now, step_now, decay_now = inputs
        state = decay_now[:, :, None, None] * state + (step_now[:, :, None] * x_now)[:, :, :, None] * b_now[:, :, None, :]
        y_now = lax.optimization_barrier(jnp.sum(state * c_now[:, :, None, :], axis=-1)) + skip_gain[None, :, None] * x_now
        return (state, y_now)
    moved = (jnp.moveaxis(x_heads, 1, 0), jnp.moveaxis(b_heads, 1, 0), jnp.moveaxis(c_heads, 1, 0), jnp.moveaxis(step, 1, 0), jnp.moveaxis(decay, 1, 0))
    final_state, outputs = lax.scan(advance, init_state, moved)
    y_all = jnp.moveaxis(outputs, 0, 1).reshape(TOKENS, H * P_SIZE)
    gated = y_all * jax.nn.silu(gate_z.astype(jnp.float32))
    per_group = gated.reshape(TOKENS, G, H // G * P_SIZE)
    scale = lax.rsqrt(lax.optimization_barrier(jnp.mean(per_group * per_group, axis=-1, keepdims=True)) + 1e-05)
    normed = ((per_group * scale).reshape(TOKENS, H * P_SIZE) * norm_gain[None, :]).astype(jnp.bfloat16)
    width = H * P_SIZE // N_TP
    total = jnp.zeros((TOKENS, D), jnp.float32)
    for block in range(N_TP):
        partial_value = jnp.dot(normed[:, block * width:(block + 1) * width], w_out[block * width:(block + 1) * width], preferred_element_type=jnp.float32).astype(jnp.bfloat16)
        partial_value = lax.optimization_barrier(partial_value)
        total = total + partial_value.astype(jnp.float32)
    mixed = total.astype(jnp.bfloat16)
    return (mixed, final_state)
```

```python
import functools

import jax
import jax.numpy as jnp
from jax import lax
from jax.experimental import pallas as pl
from jax.experimental.pallas import tpu as pltpu
from jax.sharding import Mesh
from jax.sharding import PartitionSpec as P

P_SIZE = 64
N = 256
CONV = 4
LEN = 128
HEADS = 16
CH = HEADS * P_SIZE
HALF = CH // 2
KB = 512
FAST = 48 * 1024 * 1024

F32 = jnp.float32
BF16 = jnp.bfloat16
NT = (((1,), (1,)), ((), ()))


def ring(n, step):
    return [(i, (i + step) % n) for i in range(n)]


def swap(value, axis):
    return lax.ppermute(value, axis, [(0, 1), (1, 0)])


def spread(piece):
    rows = piece.shape[0] // 2
    right = lax.ppermute(piece, "x", ring(4, 1))
    left = lax.ppermute(piece, "x", ring(4, -1))
    over = swap(piece, "yh")
    far_top = lax.ppermute(right[:rows], "x", ring(4, 1))
    far_bottom = lax.ppermute(left[rows:], "x", ring(4, -1))
    over_right = lax.ppermute(over, "x", ring(4, 1))
    over_left = lax.ppermute(over, "x", ring(4, -1))
    over_far_top = swap(far_top, "yh")
    over_far_bottom = swap(far_bottom, "yh")
    return (
        [piece, left, (far_top, far_bottom), right],
        [over, over_left, (over_far_top, over_far_bottom), over_right],
    )


def flat(pieces):
    out = []
    for row in pieces:
        for item in row:
            out.extend(item if isinstance(item, tuple) else (item,))
    return out


def kblocks():
    yh, x = lax.axis_index("yh"), lax.axis_index("x")
    return jnp.stack([((yh + dy) % 2) * 4 + (x + dx) % 4 for dy in range(2) for dx in range(4)]).astype(jnp.int32)


def project_kernel(width, steps, table, own_ref, oth_ref, *refs):
    pieces, (out_own, out_oth) = refs[:10], refs[10:]
    half = KB // 2
    stride = half + steps

    def run(hid_ref, out_ref):
        total = None
        extra = None
        at = 0
        for index in range(8):
            block = table[index]
            if index % 4 == 2:
                segments = [(pieces[at], 0), (pieces[at + 1], 0)]
                at += 2
            else:
                segments = [(pieces[at], 0), (pieces[at], stride)]
                at += 1
            for which, (ref, base) in enumerate(segments):
                start = pl.multiple_of(block * KB + which * half, half)
                hid = hid_ref[:, pl.ds(start, half)]
                term = jnp.dot(hid, ref[base : base + half, :], preferred_element_type=F32)
                total = term if total is None else total + term
                if steps:
                    term = lax.dot_general(
                        hid, ref[base + half : base + stride, :], NT, preferred_element_type=F32
                    )
                    extra = term if extra is None else extra + term
        out_ref[:, :width] = total.astype(BF16)
        if steps:
            out_ref[:, width:] = jnp.zeros((out_ref.shape[0], out_ref.shape[1] - width), BF16)
            out_ref[:, width : width + steps] = extra.astype(BF16)

    step = pl.program_id(0)
    tiles = pl.num_programs(0) // 2

    @pl.when(step < tiles)
    def _():
        run(own_ref, out_own)

    @pl.when(step >= tiles)
    def _():
        run(oth_ref, out_oth)


def project(table, own, oth, pieces, width, steps=0):
    rows, depth = own.shape
    out_width = width + (128 if steps else 0)
    tile = 256
    tiles = rows // tile

    def first(i, _):
        return (jnp.minimum(i, tiles - 1), 0)

    def second(i, _):
        return (jnp.maximum(i - tiles, 0), 0)

    return pl.pallas_call(
        functools.partial(project_kernel, width, steps),
        grid_spec=pltpu.PrefetchScalarGridSpec(
            num_scalar_prefetch=1,
            grid=(2 * tiles,),
            in_specs=[pl.BlockSpec((tile, depth), first), pl.BlockSpec((tile, depth), second)]
            + [pl.BlockSpec(p.shape, lambda i, _: (0, 0)) for p in pieces],
            out_specs=[pl.BlockSpec((tile, out_width), first), pl.BlockSpec((tile, out_width), second)],
        ),
        out_shape=[jax.ShapeDtypeStruct((rows, out_width), BF16)] * 2,
        compiler_params=pltpu.CompilerParams(vmem_limit_bytes=FAST),
        cost_estimate=pl.CostEstimate(
            flops=4 * rows * depth * width, bytes_accessed=4 * rows * depth + 2 * depth * width, transcendentals=0
        ),
        name="project",
    )(table, own, oth, *pieces)


def silu(v):
    return v / (1.0 + jnp.exp(-v))


def scan_kernel(
    info, xo, xr, bo, br, tail_x, tail_g, conv_x, conv_g, init, rate, bias, skip, y_ref, final_ref, buf_x, buf_g
):
    first = info[0] == 0
    live_to = info[1 + pl.program_id(0)]

    buf_x[8 - (CONV - 1) : 8, :] = tail_x[0].astype(F32)
    buf_g[8 - (CONV - 1) : 8, :] = tail_g[0].astype(F32)
    xo_v, xr_v = xo[...].astype(F32), xr[...].astype(F32)
    bo_v, br_v = bo[...].astype(F32), br[...].astype(F32)
    buf_x[8:, :HALF] = jnp.where(first, xo_v, xr_v)
    buf_x[8:, HALF:] = jnp.where(first, xr_v, xo_v)
    buf_g[8:, :N] = jnp.where(first, bo_v[:, :N], br_v[:, :N])
    buf_g[8:, N:] = jnp.where(first, br_v[:, :N], bo_v[:, :N])

    def conv(buf, taps_ref):
        taps = taps_ref[...].astype(F32)
        total = None
        for k in range(CONV):
            start = 8 - (CONV - 1) + k
            term = taps[k : k + 1, :] * buf[start : start + LEN, :]
            total = term if total is None else total + term
        return silu(total)

    x = conv(buf_x, conv_x)
    bc = conv(buf_g, conv_g).astype(BF16)
    b, c = bc[:, :N], bc[:, N:]

    rows = lax.broadcasted_iota(jnp.int32, (LEN, LEN), 0)
    cols = lax.broadcasted_iota(jnp.int32, (LEN, LEN), 1)
    raw = bo_v[:, N:] + br_v[:, N:] + bias[...]
    step = jnp.maximum(raw, 0.0) + jnp.log1p(jnp.exp(-jnp.abs(raw)))
    step = jnp.where((rows < live_to) & (cols < HEADS), step, 0.0)
    lower = (rows >= cols).astype(F32)
    total = jnp.dot(lower, -rate[...] * step, precision=lax.Precision.HIGHEST, preferred_element_type=F32)
    step_t = step.T
    total_t = total.T
    end_t = total_t[:, LEN - 1 : LEN]
    grow_t = jnp.exp(total_t)
    rest_t = jnp.exp(end_t - total_t) * step_t
    end = jnp.exp(end_t)

    scores = lax.dot_general(b, c, NT, preferred_element_type=F32)
    scores = jnp.where(rows <= cols, scores, 0.0)
    x_t = x.T
    init_all = init[...].reshape(CH, N)
    carried = lax.dot_general(init_all.astype(BF16), c, NT, preferred_element_type=F32)
    parts = []
    for h in range(HEADS):
        at = slice(h * P_SIZE, (h + 1) * P_SIZE)
        decay = jnp.exp(jnp.minimum(total_t[h : h + 1, :] - total[:, h : h + 1], 0.0))
        mixing = (decay * scores).astype(BF16)
        weighted = (x_t[at] * step_t[h : h + 1, :]).astype(BF16)
        inner = jnp.dot(weighted, mixing, preferred_element_type=F32)
        parts.append(inner + carried[at] * grow_t[h : h + 1, :])
        kept = (x_t[at] * rest_t[h : h + 1, :]).astype(BF16)
        final_ref[0, h] = init[0, h] * end[h : h + 1, :] + jnp.dot(kept, b, preferred_element_type=F32)
    y = jnp.concatenate(parts, axis=0).T
    y_ref[...] = y + skip[...] * x


def scan(info, xo, xr, bo, br, tail_x, tail_g, conv_x, conv_g, init, rate, bias, skip):
    rollouts = init.shape[0]

    def rows(i, _):
        return (i, 0)

    def whole(i, _):
        return (0, 0)

    return pl.pallas_call(
        scan_kernel,
        grid_spec=pltpu.PrefetchScalarGridSpec(
            num_scalar_prefetch=1,
            grid=(rollouts,),
            in_specs=[
                pl.BlockSpec((LEN, HALF), rows),
                pl.BlockSpec((LEN, HALF), rows),
                pl.BlockSpec((LEN, N + 128), rows),
                pl.BlockSpec((LEN, N + 128), rows),
                pl.BlockSpec((1, CONV - 1, CH), lambda i, _: (i, 0, 0)),
                pl.BlockSpec((1, CONV - 1, 2 * N), lambda i, _: (i, 0, 0)),
                pl.BlockSpec((CONV, CH), whole),
                pl.BlockSpec((CONV, 2 * N), whole),
                pl.BlockSpec((1, HEADS, P_SIZE, N), lambda i, _: (i, 0, 0, 0)),
                pl.BlockSpec((1, 128), whole),
                pl.BlockSpec((1, 128), whole),
                pl.BlockSpec((1, CH), whole),
            ],
            out_specs=[
                pl.BlockSpec((LEN, CH), rows),
                pl.BlockSpec((1, HEADS, P_SIZE, N), lambda i, _: (i, 0, 0, 0)),
            ],
            scratch_shapes=[pltpu.VMEM((8 + LEN, CH), F32), pltpu.VMEM((8 + LEN, 2 * N), F32)],
        ),
        out_shape=[
            jax.ShapeDtypeStruct((rollouts * LEN, CH), F32),
            jax.ShapeDtypeStruct(init.shape, F32),
        ],
        compiler_params=pltpu.CompilerParams(vmem_limit_bytes=FAST),
        cost_estimate=pl.CostEstimate(flops=2_000_000_000, bytes_accessed=14_000_000, transcendentals=4_000_000),
        name="scan",
    )(info, xo, xr, bo, br, tail_x, tail_g, conv_x, conv_g, init, rate, bias, skip)


def gate_kernel(info, y_ref, zo, zr, gain, out_ref):
    first = info[0] == 0
    zo_v, zr_v = zo[...].astype(F32), zr[...].astype(F32)
    low = y_ref[:, :HALF] * silu(jnp.where(first, zo_v, zr_v))
    high = y_ref[:, HALF:] * silu(jnp.where(first, zr_v, zo_v))
    square = jnp.sum(low * low, axis=-1, keepdims=True) + jnp.sum(high * high, axis=-1, keepdims=True)
    scale = lax.rsqrt(square * (1.0 / CH) + 1e-05)
    out_ref[:, :HALF] = (low * scale * gain[:, :HALF]).astype(BF16)
    out_ref[:, HALF:] = (high * scale * gain[:, HALF:]).astype(BF16)


def gate(info, y, zo, zr, gain):
    rows = y.shape[0] // 8

    def at(i, _):
        return (i, 0)

    return pl.pallas_call(
        gate_kernel,
        grid_spec=pltpu.PrefetchScalarGridSpec(
            num_scalar_prefetch=1,
            grid=(8,),
            in_specs=[
                pl.BlockSpec((rows, CH), at),
                pl.BlockSpec((rows, HALF), at),
                pl.BlockSpec((rows, HALF), at),
                pl.BlockSpec((1, CH), lambda i, _: (0, 0)),
            ],
            out_specs=pl.BlockSpec((rows, CH), lambda i, table: (table[1 + i], 0)),
        ),
        out_shape=jax.ShapeDtypeStruct(y.shape, BF16),
        compiler_params=pltpu.CompilerParams(vmem_limit_bytes=FAST),
        cost_estimate=pl.CostEstimate(flops=10_000_000, bytes_accessed=4_000_000, transcendentals=500_000),
        name="gate",
    )(info, y, zo, zr, gain)


def place_kernel(table, *refs):
    out_ref = refs[-1]
    for index, ref in enumerate(refs[:-1]):
        width = ref.shape[1] // 2
        for side in range(2):
            start = pl.multiple_of(table[2 * index + side] * width, width)
            out_ref[:, pl.ds(start, width)] = ref[:, side * width : (side + 1) * width]


def place(table, parts):
    rows, width = parts[0].shape
    return pl.pallas_call(
        place_kernel,
        grid_spec=pltpu.PrefetchScalarGridSpec(
            num_scalar_prefetch=1,
            grid=(1,),
            in_specs=[pl.BlockSpec((rows, width), lambda i, _: (0, 0)) for _ in parts],
            out_specs=pl.BlockSpec((rows, width * len(parts)), lambda i, _: (0, 0)),
        ),
        out_shape=jax.ShapeDtypeStruct((rows, width * len(parts)), BF16),
        compiler_params=pltpu.CompilerParams(vmem_limit_bytes=FAST),
        name="place",
    )(table, *parts)


def reduce_columns(normed, first, second):
    block = normed.shape[0] // 4
    a = jnp.dot(normed, first, preferred_element_type=F32).astype(BF16)
    b = jnp.dot(normed, second, preferred_element_type=F32).astype(BF16)

    def part(value, dz):
        return value[dz * block : (dz + 1) * block]

    far_a = lax.ppermute(part(a, 2), "z", ring(4, 1))
    far_b = lax.ppermute(part(b, 2), "z", ring(4, -1))
    up = jnp.concatenate([(part(a, 1).astype(F32) + far_a.astype(F32)).astype(BF16), part(b, 1)], axis=1)
    down = jnp.concatenate([part(a, 3), (part(b, 3).astype(F32) + far_b.astype(F32)).astype(BF16)], axis=1)
    from_below = lax.ppermute(up, "z", ring(4, 1))
    from_above = lax.ppermute(down, "z", ring(4, -1))
    mine = jnp.concatenate([part(a, 0), part(b, 0)], axis=1).astype(F32)
    mine = mine + from_below.astype(F32) + from_above.astype(F32)
    mine = mine.reshape(2, 2, block // 4, mine.shape[1])
    other = swap(mine[:, 1].astype(BF16), "yl")
    return mine[:, 0] + other.astype(F32)


def shards(
    hidden_in,
    w_gate,
    w_input,
    w_groups,
    w_step,
    w_out,
    conv_input,
    conv_groups,
    tail_input,
    tail_groups,
    init_state,
    a_rate,
    step_bias,
    skip_gain,
    norm_gain,
    offsets,
):
    yh, x, c = lax.axis_index("yh"), lax.axis_index("x"), lax.axis_index("c")
    yl, z = lax.axis_index("yl"), lax.axis_index("z")
    group = ("c", "yl", "z")
    rows = w_gate.shape[0]

    def by_owner(weight):
        width = weight.shape[1] // 16
        return weight.reshape(rows, 8, 2, width).transpose(2, 1, 0, 3).reshape(16 * rows, width)

    steps = jnp.pad(by_owner(w_step), ((0, 0), (0, 120)))
    early = jnp.concatenate([by_owner(w_groups), by_owner(w_input), steps], axis=1)
    early = lax.all_to_all(early, group, 0, 0, tiled=True)
    late = lax.all_to_all(by_owner(w_gate), group, 0, 0, tiled=True)

    step_t = early[:, N + HALF : N + HALF + 8].T
    step_t = jnp.where(
        c == 0, jnp.concatenate([step_t, jnp.zeros_like(step_t)]), jnp.concatenate([jnp.zeros_like(step_t), step_t])
    )
    half = KB // 2
    groups_piece = jnp.concatenate(
        [early[:half, :N], step_t[:, :half], early[half:, :N], step_t[:, half:]], axis=0
    )
    out_pieces = spread(w_out)
    groups_pieces = spread(groups_piece)
    input_pieces = spread(early[:, N : N + HALF])
    gate_pieces = spread(late)

    table = kblocks()
    hidden_oth = swap(hidden_in, "c")
    bc_own, bc_oth = project(table, hidden_in, hidden_oth, flat(groups_pieces), N, 16)
    bc_got = swap(bc_oth, "c")
    x_own, x_oth = project(table, hidden_in, hidden_oth, flat(input_pieces), HALF)
    x_got = swap(x_oth, "c")

    def lanes(vector):
        return jnp.pad(vector, (0, 128 - HEADS))[None, :]

    info = jnp.concatenate([jnp.reshape(c, (1,)).astype(jnp.int32), offsets])
    y, final_state = scan(
        info,
        x_own,
        x_got,
        bc_own,
        bc_got,
        tail_input,
        tail_groups,
        conv_input,
        conv_groups,
        init_state,
        lanes(a_rate),
        lanes(step_bias),
        jnp.repeat(skip_gain, P_SIZE)[None, :],
    )
    z_own, z_oth = project(table, hidden_in, hidden_oth, flat(gate_pieces), HALF)
    z_got = swap(z_oth, "c")
    at = jnp.arange(8)
    places = ((at % 4 - z) % 4) * 2 + (at // 4 + yl) % 2
    info = jnp.concatenate([jnp.reshape(c, (1,)), places]).astype(jnp.int32)
    normed = gate(info, y, z_own, z_got, norm_gain[None, :])
    normed_oth = swap(normed, "c")
    per = normed.shape[0] // 4
    normed = jnp.concatenate(
        [part[dz * per : (dz + 1) * per] for dz in range(4) for part in (normed, normed_oth)], axis=0
    )

    whole = [[None] * 4, [None] * 4]
    for dy in range(2):
        for dx in range(4):
            item = out_pieces[dy][dx]
            whole[dy][dx] = jnp.concatenate(item, axis=0) if isinstance(item, tuple) else item
    order = ((0, 0), (0, 1)), ((0, 3), (1, 0)), ((1, 1), (1, 3)), ((0, 2), (1, 2))
    sums = [reduce_columns(normed, whole[a[0]][a[1]], whole[b[0]][b[1]]) for a, b in order]
    kept = [s[0].astype(BF16) for s in sums]
    given = swap(jnp.concatenate([s[1].astype(BF16) for s in sums], axis=1), "c")
    parts = kept + [given]

    def column(dy, dx, core):
        return (((yh + dy) % 2) * 4 + (x + dx) % 4) * 2 + core

    spots = [column(*p, c) for pair in order for p in pair] + [column(*p, 1 - c) for pair in order for p in pair]
    width = kept[0].shape[1]
    given = [given[:, i * width : (i + 1) * width] for i in range(len(order))]
    mixed = place(jnp.stack(spots).astype(jnp.int32), kept + given)
    return mixed, final_state


def solution(mesh):
    fine = Mesh(mesh.devices.reshape(2, 4, 2, 2, 4), ("yh", "x", "c", "yl", "z"))
    fsdp = ("yh", "x", "c")
    tp = ("yl", "z")
    return jax.shard_map(
        shards,
        mesh=fine,
        in_specs=(
            P(fsdp, None),
            P(fsdp + tp, None),
            P(fsdp + tp, None),
            P(fsdp + tp, None),
            P(fsdp + tp, None),
            P(tp, fsdp),
            P(None, tp),
            P(None, tp),
            P(fsdp, None, tp),
            P(fsdp, None, tp),
            P(fsdp, tp, None, None),
            P(tp),
            P(tp),
            P(tp),
            P(tp),
            P(fsdp),
        ),
        out_specs=(P(fsdp + tp, None), P(fsdp, tp, None, None)),
        check_vma=False,
    )
```

```python
import functools

import jax
import jax.numpy as jnp
from jax import lax
from jax.experimental import pallas as pl
from jax.experimental.pallas import tpu as pltpu
from jax.sharding import Mesh
from jax.sharding import PartitionSpec as P

P_SIZE = 64
N = 256
CONV = 4
LEN = 128
HEADS = 16
CH = HEADS * P_SIZE
HALF = CH // 2
WIDTH = 2 * N // 2 + CH
KB = 512
FAST = 48 * 1024 * 1024

F32 = jnp.float32
BF16 = jnp.bfloat16
NT = (((1,), (1,)), ((), ()))


def ring(n, step):
    return [(i, (i + step) % n) for i in range(n)]


def swap(value, axis):
    return lax.ppermute(value, axis, [(0, 1), (1, 0)])


def after(value, *others):
    return lax.optimization_barrier((value,) + others)[0]


def right(value, *others):
    return lax.ppermute(after(value, *others), "x", ring(4, 1))


def left(value, *others):
    return lax.ppermute(after(value, *others), "x", ring(4, -1))


def over(value, *others):
    return swap(after(value, *others), "yh")


def assemble_kernel(blocks_ref, out_ref):
    out_ref[:KB, :] = blocks_ref[:, :WIDTH]
    out_ref[KB:, :] = jnp.zeros((16, WIDTH), BF16)
    steps = blocks_ref[:, WIDTH:].astype(F32).T
    out_ref[KB:, :KB] = steps[:16].astype(BF16)


def assemble(blocks):
    return pl.pallas_call(
        assemble_kernel,
        out_shape=jax.ShapeDtypeStruct((KB + 16, WIDTH), BF16),
        compiler_params=pltpu.CompilerParams(vmem_limit_bytes=16 * 1024 * 1024),
        name="assemble",
    )(blocks)


def project_kernel(steps, last, table, own_ref, oth_ref, *refs):
    pieces, refs = refs[:5], refs[5:]
    sums, refs = (refs[:2], refs[2:]) if last else ((None, None), refs)
    out_own, out_oth, weights, turned = refs
    step = pl.program_id(0)
    tiles = pl.num_programs(0) // 2
    half = KB // 2

    @pl.when(step == 0)
    def _():
        for ref, block, skip, rows in zip(pieces, (0, 1, 2, 2, 3), (0, 0, 0, half, 0), (KB, KB, half, half, KB)):
            start = pl.multiple_of(table[1 + block] * KB + skip, half)
            weights[pl.ds(start, rows), :] = ref[:rows, :]
            if steps and ref.shape[0] > rows:
                start = pl.multiple_of(table[1 + block] * KB, KB)
                turned[:, pl.ds(start, KB)] = ref[rows:, :KB]

    def run(hid_ref, sum_ref, out_ref):
        hid = hid_ref[...]
        width = weights.shape[1]
        total = jnp.dot(hid, weights[...], preferred_element_type=F32)
        if last:
            total = total + sum_ref[:, :width]
        out_ref[:, :width] = total.astype(out_ref.dtype)
        if steps:
            extra = lax.dot_general(hid, turned[...], NT, preferred_element_type=F32)
            if last:
                extra = extra + sum_ref[:, width : width + steps]
            out_ref[:, width:] = jnp.zeros((out_ref.shape[0], out_ref.shape[1] - width), out_ref.dtype)
            out_ref[:, width : width + steps] = extra.astype(out_ref.dtype)

    @pl.when(step < tiles)
    def _():
        run(own_ref, sums[0], out_own)

    @pl.when(step >= tiles)
    def _():
        run(oth_ref, sums[1], out_oth)


def project_part(own, oth, pieces, dy, steps=0, sums=()):
    rows, depth = own.shape[0], own.shape[1] // 2
    pieces = [part for piece in pieces for part in (piece if isinstance(piece, tuple) else (piece,))]
    width = pieces[0].shape[1]
    out_width = width + (128 if steps else 0)
    tile = 256
    tiles = rows // tile
    x = lax.axis_index("x")
    yh = (lax.axis_index("yh") + dy) % 2
    table = jnp.stack([yh] + [(x + dx) % 4 for dx in range(4)]).astype(jnp.int32)

    def first(i, _):
        return (jnp.minimum(i, tiles - 1), 0)

    def second(i, _):
        return (jnp.maximum(i - tiles, 0), 0)

    outs = [pl.BlockSpec((tile, out_width), first), pl.BlockSpec((tile, out_width), second)]
    return pl.pallas_call(
        functools.partial(project_kernel, steps, bool(sums)),
        grid_spec=pltpu.PrefetchScalarGridSpec(
            num_scalar_prefetch=1,
            grid=(2 * tiles,),
            in_specs=[
                pl.BlockSpec((tile, depth), lambda i, t: (jnp.minimum(i, tiles - 1), t[0])),
                pl.BlockSpec((tile, depth), lambda i, t: (jnp.maximum(i - tiles, 0), t[0])),
            ]
            + [pl.BlockSpec(p.shape, lambda i, _: (0, 0)) for p in pieces]
            + (outs if sums else []),
            out_specs=outs,
            scratch_shapes=[pltpu.VMEM((depth, width), BF16), pltpu.VMEM((16, depth), BF16)],
        ),
        out_shape=[jax.ShapeDtypeStruct((rows, out_width), BF16 if sums else F32)] * 2,
        compiler_params=pltpu.CompilerParams(vmem_limit_bytes=FAST),
        cost_estimate=pl.CostEstimate(
            flops=4 * rows * depth * width, bytes_accessed=4 * rows * depth + 2 * depth * width, transcendentals=0
        ),
        name="project",
    )(table, own, oth, *pieces, *sums)


def silu(v):
    return v / (1.0 + jnp.exp(-v))


def scan_kernel(
    info, own, got, tail_x, tail_g, conv_x, conv_g, init, rate, bias, skip, gain, out_ref, final_ref, buf_x, buf_g
):
    first = info[0] == 0
    live_to = info[1 + pl.program_id(0)]

    buf_x[8 - (CONV - 1) : 8, :] = tail_x[0].astype(F32)
    buf_g[8 - (CONV - 1) : 8, :] = tail_g[0].astype(F32)
    own_v, got_v = own[...].astype(F32), got[...].astype(F32)
    bo_v, br_v = own_v[:, :N], got_v[:, :N]
    xo_v, xr_v = own_v[:, N : N + HALF], got_v[:, N : N + HALF]
    zo_v, zr_v = own_v[:, N + HALF : WIDTH], got_v[:, N + HALF : WIDTH]
    buf_x[8:, :HALF] = jnp.where(first, xo_v, xr_v)
    buf_x[8:, HALF:] = jnp.where(first, xr_v, xo_v)
    buf_g[8:, :N] = jnp.where(first, bo_v, br_v)
    buf_g[8:, N:] = jnp.where(first, br_v, bo_v)

    def conv(buf, taps_ref):
        taps = taps_ref[...].astype(F32)
        total = None
        for k in range(CONV):
            start = 8 - (CONV - 1) + k
            term = taps[k : k + 1, :] * buf[start : start + LEN, :]
            total = term if total is None else total + term
        return silu(total)

    x = conv(buf_x, conv_x)
    bc = conv(buf_g, conv_g).astype(BF16)
    b, c = bc[:, :N], bc[:, N:]

    rows = lax.broadcasted_iota(jnp.int32, (LEN, LEN), 0)
    cols = lax.broadcasted_iota(jnp.int32, (LEN, LEN), 1)
    raw = own_v[:, WIDTH:] + got_v[:, WIDTH:] + bias[...]
    step = jnp.maximum(raw, 0.0) + jnp.log1p(jnp.exp(-jnp.abs(raw)))
    step = jnp.where((rows < live_to) & (cols < HEADS), step, 0.0)
    lower = (rows >= cols).astype(F32)
    total = jnp.dot(lower, -rate[...] * step, precision=lax.Precision.HIGHEST, preferred_element_type=F32)
    step_t = step.T
    total_t = total.T
    end_t = total_t[:, LEN - 1 : LEN]
    grow_t = jnp.exp(total_t)
    rest_t = jnp.exp(end_t - total_t) * step_t
    end = jnp.exp(end_t)

    scores = lax.dot_general(b, c, NT, preferred_element_type=F32)
    scores = jnp.where(rows <= cols, scores, 0.0)
    x_t = x.T
    init_all = init[...].reshape(CH, N)
    carried = lax.dot_general(init_all.astype(BF16), c, NT, preferred_element_type=F32)
    parts = []
    for h in range(HEADS):
        at = slice(h * P_SIZE, (h + 1) * P_SIZE)
        decay = jnp.exp(jnp.minimum(total_t[h : h + 1, :] - total[:, h : h + 1], 0.0))
        mixing = (decay * scores).astype(BF16)
        weighted = (x_t[at] * step_t[h : h + 1, :]).astype(BF16)
        inner = jnp.dot(weighted, mixing, preferred_element_type=F32)
        parts.append(inner + carried[at] * grow_t[h : h + 1, :])
        kept = (x_t[at] * rest_t[h : h + 1, :]).astype(BF16)
        final_ref[0, h] = init[0, h] * end[h : h + 1, :] + jnp.dot(kept, b, preferred_element_type=F32)
    y = jnp.concatenate(parts, axis=0).T
    y = y + skip[...] * x
    low = y[:, :HALF] * silu(jnp.where(first, zo_v, zr_v))
    high = y[:, HALF:] * silu(jnp.where(first, zr_v, zo_v))
    square = jnp.sum(low * low, axis=-1, keepdims=True) + jnp.sum(high * high, axis=-1, keepdims=True)
    scale = lax.rsqrt(square * (1.0 / CH) + 1e-05)
    low = (low * scale * gain[:, :HALF]).astype(BF16)
    high = (high * scale * gain[:, HALF:]).astype(BF16)
    for side in range(2):
        place = info[5 + 2 * pl.program_id(0) + side]
        at = pl.ds(pl.multiple_of(place * (LEN // 2), LEN // 2), LEN // 2)
        out_ref[at, :HALF] = low[side * LEN // 2 : (side + 1) * LEN // 2]
        out_ref[at, HALF:] = high[side * LEN // 2 : (side + 1) * LEN // 2]


def scan(info, own, got, tail_x, tail_g, conv_x, conv_g, init, rate, bias, skip, gain):
    rollouts = init.shape[0]

    def rows(i, _):
        return (i, 0)

    def whole(i, _):
        return (0, 0)

    return pl.pallas_call(
        scan_kernel,
        grid_spec=pltpu.PrefetchScalarGridSpec(
            num_scalar_prefetch=1,
            grid=(rollouts,),
            in_specs=[
                pl.BlockSpec((LEN, WIDTH + 128), rows),
                pl.BlockSpec((LEN, WIDTH + 128), rows),
                pl.BlockSpec((1, CONV - 1, CH), lambda i, _: (i, 0, 0)),
                pl.BlockSpec((1, CONV - 1, 2 * N), lambda i, _: (i, 0, 0)),
                pl.BlockSpec((CONV, CH), whole),
                pl.BlockSpec((CONV, 2 * N), whole),
                pl.BlockSpec((1, HEADS, P_SIZE, N), lambda i, _: (i, 0, 0, 0)),
                pl.BlockSpec((1, 128), whole),
                pl.BlockSpec((1, 128), whole),
                pl.BlockSpec((1, CH), whole),
                pl.BlockSpec((1, CH), whole),
            ],
            out_specs=[
                pl.BlockSpec((rollouts * LEN, CH), whole),
                pl.BlockSpec((1, HEADS, P_SIZE, N), lambda i, _: (i, 0, 0, 0)),
            ],
            scratch_shapes=[pltpu.VMEM((8 + LEN, CH), F32), pltpu.VMEM((8 + LEN, 2 * N), F32)],
        ),
        out_shape=[
            jax.ShapeDtypeStruct((rollouts * LEN, CH), BF16),
            jax.ShapeDtypeStruct(init.shape, F32),
        ],
        compiler_params=pltpu.CompilerParams(vmem_limit_bytes=FAST),
        cost_estimate=pl.CostEstimate(flops=2_000_000_000, bytes_accessed=14_000_000, transcendentals=4_000_000),
        name="scan",
    )(info, own, got, tail_x, tail_g, conv_x, conv_g, init, rate, bias, skip, gain)


def place_kernel(table, kept_ref, given_ref, out_ref):
    for side, ref in enumerate((kept_ref, given_ref)):
        for index in range(8):
            start = pl.multiple_of(table[8 * side + index] * N, N)
            out_ref[:, pl.ds(start, N)] = ref[:, index * N : (index + 1) * N]


def place(table, kept, given):
    rows, width = kept.shape
    return pl.pallas_call(
        place_kernel,
        grid_spec=pltpu.PrefetchScalarGridSpec(
            num_scalar_prefetch=1,
            grid=(1,),
            in_specs=[pl.BlockSpec((rows, width), lambda i, _: (0, 0))] * 2,
            out_specs=pl.BlockSpec((rows, 2 * width), lambda i, _: (0, 0)),
        ),
        out_shape=jax.ShapeDtypeStruct((rows, 2 * width), BF16),
        compiler_params=pltpu.CompilerParams(vmem_limit_bytes=FAST),
        name="place",
    )(table, kept, given)


def multiply_kernel(split, own_ref, oth_ref, *refs):
    pieces, (first_ref, second_ref, rows) = refs[:-3], refs[-3:]
    per = own_ref.shape[0] // 4
    for dz in range(4):
        for f, ref in enumerate((own_ref, oth_ref)):
            rows[(2 * dz + f) * per : (2 * dz + f + 1) * per, :] = ref[dz * per : (dz + 1) * per, :]
    depth = rows.shape[1]
    for which, out_ref in ((pieces[:split], first_ref), (pieces[split:], second_ref)):
        column = 0
        at = 0
        while at < len(which):
            ref = which[at]
            width = ref.shape[1]
            if ref.shape[0] == depth:
                total = jnp.dot(rows[...], ref[...], preferred_element_type=F32)
                at += 1
            else:
                total = jnp.dot(rows[:, : depth // 2], ref[...], preferred_element_type=F32)
                total += jnp.dot(rows[:, depth // 2 :], which[at + 1][...], preferred_element_type=F32)
                at += 2
            out_ref[:, column : column + width] = total.astype(BF16)
            column += width


def multiply(own, oth, first, second):
    rows, depth = own.shape

    def flat(pieces):
        return [part for piece in pieces for part in (piece if isinstance(piece, tuple) else (piece,))]

    def columns(pieces):
        return sum(p[0].shape[1] if isinstance(p, tuple) else p.shape[1] for p in pieces)

    total = columns(first) + columns(second)
    return pl.pallas_call(
        functools.partial(multiply_kernel, len(flat(first))),
        out_shape=[jax.ShapeDtypeStruct((2 * rows, columns(p)), BF16) for p in (first, second)],
        scratch_shapes=[pltpu.VMEM((2 * rows, depth), BF16)],
        compiler_params=pltpu.CompilerParams(vmem_limit_bytes=36 * 1024 * 1024),
        cost_estimate=pl.CostEstimate(
            flops=4 * rows * depth * total, bytes_accessed=4 * rows * depth + 2 * total * (depth + 2 * rows), transcendentals=0
        ),
        name="multiply",
    )(own, oth, *flat(first), *flat(second))


def add(*terms):
    return functools.reduce(jnp.add, [t.astype(F32) for t in terms]).astype(BF16)


def reduce_z(parts):
    far = parts(2)
    half = far.shape[1] // 2
    far_a = lax.ppermute(far[:, :half], "z", ring(4, 1))
    far_b = lax.ppermute(far[:, half:], "z", ring(4, -1))
    up, down = parts(1), parts(3)
    up = jnp.concatenate([add(up[:, :half], far_a), up[:, half:]], axis=1)
    down = jnp.concatenate([down[:, :half], add(down[:, half:], far_b)], axis=1)
    from_below = lax.ppermute(up, "z", ring(4, 1))
    from_above = lax.ppermute(down, "z", ring(4, -1))
    return add(parts(0), from_below, from_above)


def reduce_z_first(value):
    block = value.shape[0] // 4
    mine = reduce_z(lambda dz: value[dz * block : (dz + 1) * block])
    mine = mine.reshape(2, 2, block // 4, mine.shape[1])
    return add(mine[:, 0], swap(mine[:, 1], "yl"))


def reduce_yl_first(value):
    block = value.shape[0] // 16
    value = value.reshape(8, 2, block, value.shape[1])
    value = add(value[:, 0], swap(value[:, 1], "yl")).reshape(8 * block, value.shape[3])
    mine = reduce_z(lambda dz: value[dz * 2 * block : (dz + 1) * 2 * block])
    return mine.reshape(2, block, mine.shape[1])


def shards(
    hidden_in,
    w_gate,
    w_input,
    w_groups,
    w_step,
    w_out,
    conv_input,
    conv_groups,
    tail_input,
    tail_groups,
    init_state,
    a_rate,
    step_bias,
    skip_gain,
    norm_gain,
    offsets,
):
    yh, x, c = lax.axis_index("yh"), lax.axis_index("x"), lax.axis_index("c")
    yl, z = lax.axis_index("yl"), lax.axis_index("z")
    group = ("c", "yl", "z")
    rows = w_gate.shape[0]

    def by_owner(weight):
        width = weight.shape[1] // 16
        return weight.reshape(rows, 8, 2, width).transpose(2, 1, 0, 3).reshape(16 * rows, width)

    steps = by_owner(w_step).reshape(2, 8 * rows, 8)
    steps = jnp.concatenate([jnp.pad(steps[core], ((0, 0), (8 * core, 120 - 8 * core))) for core in range(2)])
    blocks = jnp.concatenate([by_owner(w_groups), by_owner(w_input), by_owner(w_gate), steps], axis=1)
    s_own = assemble(lax.all_to_all(blocks, group, 0, 0, tiled=True))
    hidden_oth = swap(hidden_in, "c")

    half = KB // 2
    w_r, w_l, w_o = right(w_out), left(w_out), over(w_out)
    s_r, s_l, s_o = right(s_own, w_r, w_l), left(s_own, w_r, w_l), over(s_own, w_o)
    s_ft, s_fb = right(s_r[:half], s_l), left(s_l[half:], s_r)
    near = project_part(hidden_in, hidden_oth, [s_own, s_l, (s_ft, s_fb), s_r], 0, 16)
    s_or, s_ol = right(s_o, s_ft, s_fb), left(s_o, s_ft, s_fb)
    s_oft, s_ofb = over(s_ft), over(s_fb)
    own, oth = project_part(hidden_in, hidden_oth, [s_o, s_ol, (s_oft, s_ofb), s_or], 1, 16, near)
    w_ft, w_fb = right(w_r[:KB], s_or, s_ol), left(w_l[KB:], s_or, s_ol)
    w_or, w_ol = right(w_o, s_or, s_ol), left(w_o, s_or, s_ol)
    w_oft, w_ofb = over(w_ft, s_oft, s_ofb), over(w_fb, s_oft, s_ofb)
    got = swap(after(oth, w_ft, w_fb), "c")

    def lanes(vector):
        return jnp.pad(vector, (0, 128 - HEADS))[None, :]

    at = jnp.arange(8)
    places = ((at % 4 - z) % 4) * 2 + (at // 4 + yl) % 2
    normed, final_state = scan(
        jnp.concatenate([jnp.reshape(c, (1,)), offsets, places]).astype(jnp.int32),
        own,
        got,
        tail_input,
        tail_groups,
        conv_input,
        conv_groups,
        init_state,
        lanes(a_rate),
        lanes(step_bias),
        jnp.repeat(skip_gain, P_SIZE)[None, :],
        norm_gain[None, :],
    )
    normed_oth = swap(after(normed, w_or, w_ol, w_oft, w_ofb), "c")

    first, second = multiply(
        normed, normed_oth, [w_out, w_l, w_r, w_o], [(w_ft, w_fb), w_ol, (w_oft, w_ofb), w_or]
    )
    first, second = reduce_yl_first(first), reduce_z_first(second)
    sums = jnp.concatenate([first, second], axis=2)
    kept = sums[0]
    given = swap(sums[1], "c")

    order = [((yh + dy) % 2) * 4 + (x + dx) % 4 for dy, dx in ((0, 0), (0, 1), (0, 3), (1, 0), (0, 2), (1, 1), (1, 2), (1, 3))]
    mixed = place(jnp.stack([2 * p + core for core in (c, 1 - c) for p in order]).astype(jnp.int32), kept, given)
    return mixed, final_state


def solution(mesh):
    fine = Mesh(mesh.devices.reshape(2, 4, 2, 2, 4), ("yh", "x", "c", "yl", "z"))
    fsdp = ("yh", "x", "c")
    tp = ("yl", "z")
    return jax.shard_map(
        shards,
        mesh=fine,
        in_specs=(
            P(fsdp, None),
            P(fsdp + tp, None),
            P(fsdp + tp, None),
            P(fsdp + tp, None),
            P(fsdp + tp, None),
            P(tp, fsdp),
            P(None, tp),
            P(None, tp),
            P(fsdp, None, tp),
            P(fsdp, None, tp),
            P(fsdp, tp, None, None),
            P(tp),
            P(tp),
            P(tp),
            P(tp),
            P(fsdp),
        ),
        out_specs=(P(fsdp + tp, None), P(fsdp, tp, None, None)),
        check_vma=False,
    )
```

```python
import functools

import jax
import jax.numpy as jnp
from jax import lax
from jax.experimental import pallas as pl
from jax.experimental.pallas import tpu as pltpu
from jax.sharding import Mesh
from jax.sharding import PartitionSpec as P

P_SIZE = 64
N = 256
CONV = 4
LEN = 128
HEADS = 16
CH = HEADS * P_SIZE
HALF = CH // 2
WIDTH = 2 * N // 2 + CH
KB = 512
FAST = 48 * 1024 * 1024

F32 = jnp.float32
BF16 = jnp.bfloat16
NT = (((1,), (1,)), ((), ()))


def ring(n, step):
    return [(i, (i + step) % n) for i in range(n)]


def swap(value, axis):
    return lax.ppermute(value, axis, [(0, 1), (1, 0)])


def after(value, *others):
    return lax.optimization_barrier((value,) + others)[0]


def right(value, *others):
    return lax.ppermute(after(value, *others), "x", ring(4, 1))


def left(value, *others):
    return lax.ppermute(after(value, *others), "x", ring(4, -1))


def over(value, *others):
    return swap(after(value, *others), "yh")


def deal_kernel(groups_ref, input_ref, gate_ref, step_ref, out_ref):
    rows = groups_ref.shape[0]
    lanes = lax.broadcasted_iota(jnp.int32, (rows, 128), 1)
    steps = step_ref[...].astype(F32)
    for core in range(2):
        for t in range(8):
            here = slice((8 * core + t) * rows, (8 * core + t + 1) * rows)
            column = 0
            for ref in (groups_ref, input_ref, gate_ref):
                width = ref.shape[1] // 16
                first = (2 * t + core) * width
                out_ref[here, column : column + width] = ref[:, first : first + width]
                column += width
            turned = pltpu.roll(steps, (128 - HEADS * t) % 128, 1) if t else steps
            mine = (lanes >= 8 * core) & (lanes < 8 * core + 8)
            out_ref[here, column:] = jnp.where(mine, turned, 0.0).astype(BF16)


def deal(groups, inputs, gates, steps):
    return pl.pallas_call(
        deal_kernel,
        out_shape=jax.ShapeDtypeStruct((16 * groups.shape[0], WIDTH + 128), BF16),
        compiler_params=pltpu.CompilerParams(vmem_limit_bytes=16 * 1024 * 1024),
        name="deal",
    )(groups, inputs, gates, steps)


def assemble_kernel(blocks_ref, out_ref):
    out_ref[:KB, :] = blocks_ref[:, :WIDTH]
    out_ref[KB:, :] = jnp.zeros((16, WIDTH), BF16)
    steps = blocks_ref[:, WIDTH:].astype(F32).T
    out_ref[KB:, :KB] = steps[:16].astype(BF16)


def assemble(blocks):
    return pl.pallas_call(
        assemble_kernel,
        out_shape=jax.ShapeDtypeStruct((KB + 16, WIDTH), BF16),
        compiler_params=pltpu.CompilerParams(vmem_limit_bytes=16 * 1024 * 1024),
        name="assemble",
    )(blocks)


def project_kernel(steps, counts, last, table, own_hbm, oth_hbm, *refs):
    pieces, refs = list(refs[: sum(counts)]), refs[sum(counts) :]
    parts = [[pieces.pop(0) for _ in range(count)] for count in counts]
    final = len(parts) - 1
    sums, refs = (refs[:2], refs[2:]) if last else ((), refs)
    outs, (hid, weights, totals, results, sems) = refs[:2], refs[2:]
    rows = own_hbm.shape[0]
    width = weights.shape[2]
    half = KB // 2
    fetches = []
    for at, part in enumerate(parts):
        start = pl.multiple_of(table[at] * KB, KB)
        copies = [
            pltpu.make_async_copy(src.at[:, pl.ds(start, KB)], hid.at[at, which], sems.at[at, which])
            for which, src in enumerate((own_hbm, oth_hbm))
        ]
        for which, src in enumerate(part):
            into = weights.at[at, pl.ds(which * half, src.shape[0])]
            copies.append(pltpu.make_async_copy(src, into, sems.at[at, 2 + which]))
        fetches.append(copies)
        for copy in copies:
            copy.start()
    if last:
        fetches.append([pltpu.make_async_copy(src, totals.at[1, which], sems.at[len(parts), which]) for which, src in enumerate(sums)])
        for copy in fetches[-1]:
            copy.start()
    tile = 256
    stores = []
    for at in range(len(parts)):
        for copy in fetches[at]:
            copy.wait()
        if last and at == final:
            for copy in fetches[-1]:
                copy.wait()
        for which in (1, 0):
            for first in range(0, rows, tile):
                here = pl.ds(first, tile)
                block = hid[at, which, here]
                main = jnp.dot(block, weights[at, :KB], preferred_element_type=F32)
                extra = lax.dot_general(block, weights[at, KB:, :KB], NT, preferred_element_type=F32)
                extra = jnp.concatenate([extra, jnp.zeros((tile, 128 - steps), F32)], axis=1)
                if at:
                    main += totals[0, which, here, :width]
                    extra += totals[0, which, here, width:]
                if at < final:
                    totals[0, which, here, :width] = main
                    totals[0, which, here, width:] = extra
                else:
                    if last:
                        main += totals[1, which, here, :width]
                        extra += totals[1, which, here, width:]
                    results[which, here, :width] = main.astype(results.dtype)
                    results[which, here, width:] = extra.astype(results.dtype)
            if at == final:
                stores.append(pltpu.make_async_copy(results.at[which], outs[which], sems.at[len(parts) + 1, which]))
                stores[-1].start()
    for store in stores:
        store.wait()


def project_part(own, oth, pieces, steps, sums=()):
    rows, depth = own.shape
    x, yh = lax.axis_index("x"), lax.axis_index("yh")
    table = jnp.stack([4 * ((yh + dy) % 2) + (x + dx) % 4 for (dy, dx), _ in pieces]).astype(jnp.int32)
    pieces = [piece if isinstance(piece, tuple) else (piece,) for _, piece in pieces]
    counts = [len(piece) for piece in pieces]
    pieces = [part for piece in pieces for part in piece]
    width = pieces[0].shape[1]
    out_width = width + 128
    dtype = BF16 if sums else F32
    return pl.pallas_call(
        functools.partial(project_kernel, steps, counts, bool(sums)),
        grid_spec=pltpu.PrefetchScalarGridSpec(
            num_scalar_prefetch=1,
            grid=(1,),
            in_specs=[pl.BlockSpec(memory_space=pl.ANY)] * (2 + len(pieces) + len(sums)),
            out_specs=[pl.BlockSpec(memory_space=pl.ANY)] * 2,
            scratch_shapes=[
                pltpu.VMEM((len(counts), 2, rows, KB), BF16),
                pltpu.VMEM((len(counts), KB + 16, width), BF16),
                pltpu.VMEM((2 if sums else 1, 2, rows, out_width), F32),
                pltpu.VMEM((2, rows, out_width), dtype),
                pltpu.SemaphoreType.DMA((len(counts) + 2, 4)),
            ],
        ),
        out_shape=[jax.ShapeDtypeStruct((rows, out_width), dtype)] * 2,
        compiler_params=pltpu.CompilerParams(vmem_limit_bytes=FAST),
        cost_estimate=pl.CostEstimate(
            flops=4 * rows * KB * width * len(counts),
            bytes_accessed=2 * KB * (2 * rows + width) * len(counts) + 12 * rows * width,
            transcendentals=0,
        ),
        name="project",
    )(table, own, oth, *pieces, *sums)


def silu(v):
    return v / (1.0 + jnp.exp(-v))


def scan_kernel(
    info, own, got, tail_x, tail_g, conv_x, conv_g, init, rate, bias, skip, gain, out_ref, final_ref, buf_x, buf_g
):
    first = info[0] == 0
    live_to = info[1 + pl.program_id(0)]

    buf_x[8 - (CONV - 1) : 8, :] = tail_x[0].astype(F32)
    buf_g[8 - (CONV - 1) : 8, :] = tail_g[0].astype(F32)
    own_v, got_v = own[...].astype(F32), got[...].astype(F32)
    bo_v, br_v = own_v[:, :N], got_v[:, :N]
    xo_v, xr_v = own_v[:, N : N + HALF], got_v[:, N : N + HALF]
    zo_v, zr_v = own_v[:, N + HALF : WIDTH], got_v[:, N + HALF : WIDTH]
    buf_x[8:, :HALF] = jnp.where(first, xo_v, xr_v)
    buf_x[8:, HALF:] = jnp.where(first, xr_v, xo_v)
    buf_g[8:, :N] = jnp.where(first, bo_v, br_v)
    buf_g[8:, N:] = jnp.where(first, br_v, bo_v)

    def conv(buf, taps_ref):
        taps = taps_ref[...].astype(F32)
        total = None
        for k in range(CONV):
            start = 8 - (CONV - 1) + k
            term = taps[k : k + 1, :] * buf[start : start + LEN, :]
            total = term if total is None else total + term
        return silu(total)

    x = conv(buf_x, conv_x)
    bc = conv(buf_g, conv_g).astype(BF16)
    b, c = bc[:, :N], bc[:, N:]

    rows = lax.broadcasted_iota(jnp.int32, (LEN, LEN), 0)
    cols = lax.broadcasted_iota(jnp.int32, (LEN, LEN), 1)
    raw = own_v[:, WIDTH:] + got_v[:, WIDTH:] + bias[...]
    step = jnp.maximum(raw, 0.0) + jnp.log1p(jnp.exp(-jnp.abs(raw)))
    step = jnp.where((rows < live_to) & (cols < HEADS), step, 0.0)
    lower = (rows >= cols).astype(F32)
    total = jnp.dot(lower, -rate[...] * step, precision=lax.Precision.HIGHEST, preferred_element_type=F32)
    step_t = step.T
    total_t = total.T
    end_t = total_t[:, LEN - 1 : LEN]
    grow_t = jnp.exp(total_t)
    rest_t = jnp.exp(end_t - total_t) * step_t
    end = jnp.exp(end_t)

    scores = lax.dot_general(b, c, NT, preferred_element_type=F32)
    scores = jnp.where(rows <= cols, scores, 0.0)
    x_t = x.T
    init_all = init[...].reshape(CH, N)
    carried = lax.dot_general(init_all.astype(BF16), c, NT, preferred_element_type=F32)
    parts, kept = [], []
    for h in range(HEADS):
        at = slice(h * P_SIZE, (h + 1) * P_SIZE)
        decay = jnp.exp(jnp.minimum(total_t[h : h + 1, :] - total[:, h : h + 1], 0.0))
        mixing = (decay * scores).astype(BF16)
        weighted = (x_t[at] * step_t[h : h + 1, :]).astype(BF16)
        inner = jnp.dot(weighted, mixing, preferred_element_type=F32)
        parts.append(inner + carried[at] * grow_t[h : h + 1, :])
        kept.append((x_t[at] * rest_t[h : h + 1, :]).astype(BF16))
    added = jnp.dot(jnp.concatenate(kept, axis=0), b, preferred_element_type=F32)
    for h in range(HEADS):
        final_ref[0, h] = init[0, h] * end[h : h + 1, :] + added[h * P_SIZE : (h + 1) * P_SIZE]
    y = jnp.concatenate(parts, axis=0).T
    y = y + skip[...] * x
    low = y[:, :HALF] * silu(jnp.where(first, zo_v, zr_v))
    high = y[:, HALF:] * silu(jnp.where(first, zr_v, zo_v))
    square = jnp.sum(low * low, axis=-1, keepdims=True) + jnp.sum(high * high, axis=-1, keepdims=True)
    scale = lax.rsqrt(square * (1.0 / CH) + 1e-05)
    low = (low * scale * gain[:, :HALF]).astype(BF16)
    high = (high * scale * gain[:, HALF:]).astype(BF16)
    for side in range(2):
        place = info[5 + 2 * pl.program_id(0) + side]
        at = pl.ds(pl.multiple_of(place * (LEN // 2), LEN // 2), LEN // 2)
        out_ref[at, :HALF] = low[side * LEN // 2 : (side + 1) * LEN // 2]
        out_ref[at, HALF:] = high[side * LEN // 2 : (side + 1) * LEN // 2]


def scan(info, own, got, tail_x, tail_g, conv_x, conv_g, init, rate, bias, skip, gain):
    rollouts = init.shape[0]

    def rows(i, _):
        return (i, 0)

    def whole(i, _):
        return (0, 0)

    return pl.pallas_call(
        scan_kernel,
        grid_spec=pltpu.PrefetchScalarGridSpec(
            num_scalar_prefetch=1,
            grid=(rollouts,),
            in_specs=[
                pl.BlockSpec((LEN, WIDTH + 128), rows),
                pl.BlockSpec((LEN, WIDTH + 128), rows),
                pl.BlockSpec((1, CONV - 1, CH), lambda i, _: (i, 0, 0)),
                pl.BlockSpec((1, CONV - 1, 2 * N), lambda i, _: (i, 0, 0)),
                pl.BlockSpec((CONV, CH), whole),
                pl.BlockSpec((CONV, 2 * N), whole),
                pl.BlockSpec((1, HEADS, P_SIZE, N), lambda i, _: (i, 0, 0, 0)),
                pl.BlockSpec((1, 128), whole),
                pl.BlockSpec((1, 128), whole),
                pl.BlockSpec((1, CH), whole),
                pl.BlockSpec((1, CH), whole),
            ],
            out_specs=[
                pl.BlockSpec((rollouts * LEN, CH), whole),
                pl.BlockSpec((1, HEADS, P_SIZE, N), lambda i, _: (i, 0, 0, 0)),
            ],
            scratch_shapes=[pltpu.VMEM((8 + LEN, CH), F32), pltpu.VMEM((8 + LEN, 2 * N), F32)],
        ),
        out_shape=[
            jax.ShapeDtypeStruct((rollouts * LEN, CH), BF16),
            jax.ShapeDtypeStruct(init.shape, F32),
        ],
        compiler_params=pltpu.CompilerParams(vmem_limit_bytes=FAST),
        cost_estimate=pl.CostEstimate(flops=2_000_000_000, bytes_accessed=14_000_000, transcendentals=4_000_000),
        name="scan",
    )(info, own, got, tail_x, tail_g, conv_x, conv_g, init, rate, bias, skip, gain)


def place_kernel(table, kept_ref, given_ref, out_ref):
    for side, ref in enumerate((kept_ref, given_ref)):
        for index in range(8):
            start = pl.multiple_of(table[8 * side + index] * N, N)
            out_ref[:, pl.ds(start, N)] = ref[:, index * N : (index + 1) * N]


def place(table, kept, given):
    rows, width = kept.shape
    return pl.pallas_call(
        place_kernel,
        grid_spec=pltpu.PrefetchScalarGridSpec(
            num_scalar_prefetch=1,
            grid=(1,),
            in_specs=[pl.BlockSpec((rows, width), lambda i, _: (0, 0))] * 2,
            out_specs=pl.BlockSpec((rows, 2 * width), lambda i, _: (0, 0)),
        ),
        out_shape=jax.ShapeDtypeStruct((rows, 2 * width), BF16),
        compiler_params=pltpu.CompilerParams(vmem_limit_bytes=FAST),
        name="place",
    )(table, kept, given)


def multiply_kernel(split, own_ref, oth_ref, *refs):
    pieces, (first_ref, second_ref, rows) = refs[:-3], refs[-3:]
    per = own_ref.shape[0] // 4
    for dz in range(4):
        for f, ref in enumerate((own_ref, oth_ref)):
            rows[(2 * dz + f) * per : (2 * dz + f + 1) * per, :] = ref[dz * per : (dz + 1) * per, :]
    width = pieces[0].shape[1]
    for at, ref in enumerate(pieces):
        out_ref, column = (first_ref, at * width) if at < split else (second_ref, (at - split) * width)
        total = jnp.dot(rows[...], ref[...], preferred_element_type=F32)
        out_ref[:, column : column + width] = total.astype(BF16)


def multiply(own, oth, first, second):
    rows, depth = own.shape
    columns = [len(pieces) * pieces[0].shape[1] for pieces in (first, second)]
    total = sum(columns)
    return pl.pallas_call(
        functools.partial(multiply_kernel, len(first)),
        out_shape=[jax.ShapeDtypeStruct((2 * rows, n), BF16) for n in columns],
        scratch_shapes=[pltpu.VMEM((2 * rows, depth), BF16)],
        compiler_params=pltpu.CompilerParams(vmem_limit_bytes=36 * 1024 * 1024),
        cost_estimate=pl.CostEstimate(
            flops=4 * rows * depth * total, bytes_accessed=4 * rows * depth + 2 * total * (depth + 2 * rows), transcendentals=0
        ),
        name="multiply",
    )(own, oth, *first, *second)


def add(*terms):
    return functools.reduce(jnp.add, [t.astype(F32) for t in terms]).astype(BF16)


def reduce_z(parts):
    far = parts(2)
    half = far.shape[1] // 2
    far_a = lax.ppermute(far[:, :half], "z", ring(4, 1))
    far_b = lax.ppermute(far[:, half:], "z", ring(4, -1))
    up, down = parts(1), parts(3)
    up = jnp.concatenate([add(up[:, :half], far_a), up[:, half:]], axis=1)
    down = jnp.concatenate([down[:, :half], add(down[:, half:], far_b)], axis=1)
    from_below = lax.ppermute(up, "z", ring(4, 1))
    from_above = lax.ppermute(down, "z", ring(4, -1))
    return add(parts(0), from_below, from_above)


def reduce_z_first(value):
    block = value.shape[0] // 4
    mine = reduce_z(lambda dz: value[dz * block : (dz + 1) * block])
    mine = mine.reshape(2, 2, block // 4, mine.shape[1])
    return add(mine[:, 0], swap(mine[:, 1], "yl"))


def reduce_yl_first(value):
    block = value.shape[0] // 16
    value = value.reshape(8, 2, block, value.shape[1])
    value = add(value[:, 0], swap(value[:, 1], "yl")).reshape(8 * block, value.shape[3])
    mine = reduce_z(lambda dz: value[dz * 2 * block : (dz + 1) * 2 * block])
    return mine.reshape(2, block, mine.shape[1])


def shards(
    hidden_in,
    w_gate,
    w_input,
    w_groups,
    w_step,
    w_out,
    conv_input,
    conv_groups,
    tail_input,
    tail_groups,
    init_state,
    a_rate,
    step_bias,
    skip_gain,
    norm_gain,
    offsets,
):
    yh, x, c = lax.axis_index("yh"), lax.axis_index("x"), lax.axis_index("c")
    yl, z = lax.axis_index("yl"), lax.axis_index("z")
    group = ("c", "yl", "z")
    blocks = deal(w_groups, w_input, w_gate, w_step)
    s_own = assemble(lax.all_to_all(blocks, group, 0, 0, tiled=True))
    hidden_oth = swap(hidden_in, "c")

    half = KB // 2
    w_r, w_l = right(w_out), left(w_out)
    w_f = lax.ppermute(w_out, "x", ring(4, 2))
    s_r, s_l, s_o = right(s_own, w_r, w_l, w_f), left(s_own, w_r, w_l, w_f), over(s_own)
    w_o = over(w_out, s_o)
    s_ft, s_fb = right(s_r[:half], s_l), left(s_l[half:], s_r)
    near = project_part(
        hidden_in,
        hidden_oth,
        [((0, 0), s_own), ((0, 1), s_l), ((0, 3), s_r), ((1, 0), s_o), ((0, 2), (s_ft, s_fb))],
        16,
    )
    s_or, s_ol = right(s_o, s_ft, s_fb, w_o), left(s_o, s_ft, s_fb, w_o)
    s_oft, s_ofb = over(s_ft), over(s_fb)
    own, oth = project_part(
        hidden_in, hidden_oth, [((1, 1), s_ol), ((1, 3), s_or), ((1, 2), (s_oft, s_ofb))], 16, near
    )
    w_or, w_ol, w_of = right(w_o, s_or, s_ol), left(w_o, s_or, s_ol), over(w_f, s_oft, s_ofb)
    got = swap(oth, "c")

    def lanes(vector):
        return jnp.pad(vector, (0, 128 - HEADS))[None, :]

    at = jnp.arange(8)
    places = ((at % 4 - z) % 4) * 2 + (at // 4 + yl) % 2
    normed, final_state = scan(
        jnp.concatenate([jnp.reshape(c, (1,)), offsets, places]).astype(jnp.int32),
        own,
        got,
        tail_input,
        tail_groups,
        conv_input,
        conv_groups,
        init_state,
        lanes(a_rate),
        lanes(step_bias),
        jnp.repeat(skip_gain, P_SIZE)[None, :],
        norm_gain[None, :],
    )
    normed_oth = swap(after(normed, w_or, w_ol, w_of), "c")

    first, second = multiply(normed, normed_oth, [w_out, w_l, w_r, w_o], [w_f, w_ol, w_of, w_or])
    first, second = reduce_yl_first(first), reduce_z_first(second)
    sums = jnp.concatenate([first, second], axis=2)
    kept = sums[0]
    given = swap(sums[1], "c")

    order = [((yh + dy) % 2) * 4 + (x + dx) % 4 for dy, dx in ((0, 0), (0, 1), (0, 3), (1, 0), (0, 2), (1, 1), (1, 2), (1, 3))]
    mixed = place(jnp.stack([2 * p + core for core in (c, 1 - c) for p in order]).astype(jnp.int32), kept, given)
    return mixed, final_state


def solution(mesh):
    fine = Mesh(mesh.devices.reshape(2, 4, 2, 2, 4), ("yh", "x", "c", "yl", "z"))
    fsdp = ("yh", "x", "c")
    tp = ("yl", "z")
    return jax.shard_map(
        shards,
        mesh=fine,
        in_specs=(
            P(fsdp, None),
            P(fsdp + tp, None),
            P(fsdp + tp, None),
            P(fsdp + tp, None),
            P(fsdp + tp, None),
            P(tp, fsdp),
            P(None, tp),
            P(None, tp),
            P(fsdp, None, tp),
            P(fsdp, None, tp),
            P(fsdp, tp, None, None),
            P(tp),
            P(tp),
            P(tp),
            P(tp),
            P(fsdp),
        ),
        out_specs=(P(fsdp + tp, None), P(fsdp, tp, None, None)),
        check_vma=False,
    )
```

```python
import functools

import jax
import jax.numpy as jnp
from jax import lax
from jax.experimental import pallas as pl
from jax.experimental.pallas import tpu as pltpu
from jax.sharding import Mesh
from jax.sharding import PartitionSpec as P

P_SIZE = 64
N = 256
CONV = 4
LEN = 128
HEADS = 16
CH = HEADS * P_SIZE
HALF = CH // 2
WIDTH = 2 * N // 2 + CH
KB = 512
FAST = 48 * 1024 * 1024

F32 = jnp.float32
BF16 = jnp.bfloat16
NT = (((1,), (1,)), ((), ()))


def ring(n, step):
    return [(i, (i + step) % n) for i in range(n)]


def swap(value, axis):
    return lax.ppermute(value, axis, [(0, 1), (1, 0)])


def after(value, *others):
    return lax.optimization_barrier((value,) + others)[0]


def right(value, *others):
    return lax.ppermute(after(value, *others), "x", ring(4, 1))


def left(value, *others):
    return lax.ppermute(after(value, *others), "x", ring(4, -1))


def over(value, *others):
    return swap(after(value, *others), "yh")


def deal_kernel(groups_ref, input_ref, gate_ref, step_ref, out_ref):
    rows = groups_ref.shape[0]
    lanes = lax.broadcasted_iota(jnp.int32, (rows, 128), 1)
    steps = step_ref[...].astype(F32)
    for core in range(2):
        for t in range(8):
            here = slice((8 * core + t) * rows, (8 * core + t + 1) * rows)
            column = 0
            for ref in (groups_ref, input_ref, gate_ref):
                width = ref.shape[1] // 16
                first = (2 * t + core) * width
                out_ref[here, column : column + width] = ref[:, first : first + width]
                column += width
            turned = pltpu.roll(steps, (128 - HEADS * t) % 128, 1) if t else steps
            mine = (lanes >= 8 * core) & (lanes < 8 * core + 8)
            out_ref[here, column:] = jnp.where(mine, turned, 0.0).astype(BF16)


def deal(groups, inputs, gates, steps):
    return pl.pallas_call(
        deal_kernel,
        out_shape=jax.ShapeDtypeStruct((16 * groups.shape[0], WIDTH + 128), BF16),
        compiler_params=pltpu.CompilerParams(vmem_limit_bytes=60 * 1024 * 1024),
        name="deal",
    )(groups, inputs, gates, steps)


def assemble_kernel(blocks_ref, out_ref):
    out_ref[:KB, :] = blocks_ref[:, :WIDTH]
    out_ref[KB:, :] = jnp.zeros((16, WIDTH), BF16)
    steps = blocks_ref[:, WIDTH:].astype(F32).T
    out_ref[KB:, :KB] = steps[:16].astype(BF16)


def assemble(blocks):
    return pl.pallas_call(
        assemble_kernel,
        out_shape=jax.ShapeDtypeStruct((KB + 16, WIDTH), BF16),
        compiler_params=pltpu.CompilerParams(vmem_limit_bytes=16 * 1024 * 1024),
        name="assemble",
    )(blocks)


def project_kernel(steps, counts, last, table, own_hbm, oth_hbm, *refs):
    pieces, refs = list(refs[: sum(counts)]), refs[sum(counts) :]
    parts = [[pieces.pop(0) for _ in range(count)] for count in counts]
    final = len(parts) - 1
    sums, refs = (refs[:2], refs[2:]) if last else ((), refs)
    outs, (hid, weights, totals, results, sems) = refs[:2], refs[2:]
    rows = own_hbm.shape[0]
    width = weights.shape[2]
    half = KB // 2
    fetches = []
    for at, part in enumerate(parts):
        start = pl.multiple_of(table[at] * KB, KB)
        copies = [
            pltpu.make_async_copy(src.at[:, pl.ds(start, KB)], hid.at[at, which], sems.at[at, which])
            for which, src in enumerate((own_hbm, oth_hbm))
        ]
        for which, src in enumerate(part):
            into = weights.at[at, pl.ds(which * half, src.shape[0])]
            copies.append(pltpu.make_async_copy(src, into, sems.at[at, 2 + which]))
        fetches.append(copies)
        for copy in copies:
            copy.start()
    if last:
        fetches.append([pltpu.make_async_copy(src, totals.at[1, which], sems.at[len(parts), which]) for which, src in enumerate(sums)])
        for copy in fetches[-1]:
            copy.start()
    tile = 256
    stores = []
    for at in range(len(parts)):
        for copy in fetches[at]:
            copy.wait()
        if last and at == final:
            for copy in fetches[-1]:
                copy.wait()
        for which in (1, 0):
            for first in range(0, rows, tile):
                here = pl.ds(first, tile)
                block = hid[at, which, here]
                main = jnp.dot(block, weights[at, :KB], preferred_element_type=F32)
                extra = lax.dot_general(block, weights[at, KB:, :KB], NT, preferred_element_type=F32)
                extra = jnp.concatenate([extra, jnp.zeros((tile, 128 - steps), F32)], axis=1)
                if at:
                    main += totals[0, which, here, :width]
                    extra += totals[0, which, here, width:]
                if at < final:
                    totals[0, which, here, :width] = main
                    totals[0, which, here, width:] = extra
                else:
                    if last:
                        main += totals[1, which, here, :width]
                        extra += totals[1, which, here, width:]
                    results[which, here, :width] = main.astype(results.dtype)
                    results[which, here, width:] = extra.astype(results.dtype)
            if at == final:
                stores.append(pltpu.make_async_copy(results.at[which], outs[which], sems.at[len(parts) + 1, which]))
                stores[-1].start()
    for store in stores:
        store.wait()


def project_part(own, oth, pieces, steps, sums=()):
    rows, depth = own.shape
    x, yh = lax.axis_index("x"), lax.axis_index("yh")
    table = jnp.stack([4 * ((yh + dy) % 2) + (x + dx) % 4 for (dy, dx), _ in pieces]).astype(jnp.int32)
    pieces = [piece if isinstance(piece, tuple) else (piece,) for _, piece in pieces]
    counts = [len(piece) for piece in pieces]
    pieces = [part for piece in pieces for part in piece]
    width = pieces[0].shape[1]
    out_width = width + 128
    dtype = BF16 if sums else F32
    return pl.pallas_call(
        functools.partial(project_kernel, steps, counts, bool(sums)),
        grid_spec=pltpu.PrefetchScalarGridSpec(
            num_scalar_prefetch=1,
            grid=(1,),
            in_specs=[pl.BlockSpec(memory_space=pl.ANY)] * (2 + len(pieces) + len(sums)),
            out_specs=[pl.BlockSpec(memory_space=pl.ANY)] * 2,
            scratch_shapes=[
                pltpu.VMEM((len(counts), 2, rows, KB), BF16),
                pltpu.VMEM((len(counts), KB + 16, width), BF16),
                pltpu.VMEM((2 if sums else 1, 2, rows, out_width), F32),
                pltpu.VMEM((2, rows, out_width), dtype),
                pltpu.SemaphoreType.DMA((len(counts) + 2, 4)),
            ],
        ),
        out_shape=[jax.ShapeDtypeStruct((rows, out_width), dtype)] * 2,
        compiler_params=pltpu.CompilerParams(vmem_limit_bytes=FAST),
        cost_estimate=pl.CostEstimate(
            flops=4 * rows * KB * width * len(counts),
            bytes_accessed=2 * KB * (2 * rows + width) * len(counts) + 12 * rows * width,
            transcendentals=0,
        ),
        name="project",
    )(table, own, oth, *pieces, *sums)


def silu(v):
    return v / (1.0 + jnp.exp(-v))


def scan_kernel(
    info, own, got, tail_x, tail_g, conv_x, conv_g, init, rate, bias, skip, gain, out_ref, final_ref, buf_x, buf_g
):
    first = info[0] == 0
    live_to = info[1 + pl.program_id(0)]

    buf_x[8 - (CONV - 1) : 8, :] = tail_x[0].astype(F32)
    buf_g[8 - (CONV - 1) : 8, :] = tail_g[0].astype(F32)
    own_v, got_v = own[...].astype(F32), got[...].astype(F32)
    bo_v, br_v = own_v[:, :N], got_v[:, :N]
    xo_v, xr_v = own_v[:, N : N + HALF], got_v[:, N : N + HALF]
    zo_v, zr_v = own_v[:, N + HALF : WIDTH], got_v[:, N + HALF : WIDTH]
    buf_x[8:, :HALF] = jnp.where(first, xo_v, xr_v)
    buf_x[8:, HALF:] = jnp.where(first, xr_v, xo_v)
    buf_g[8:, :N] = jnp.where(first, bo_v, br_v)
    buf_g[8:, N:] = jnp.where(first, br_v, bo_v)

    def conv(buf, taps_ref):
        taps = taps_ref[...].astype(F32)
        total = None
        for k in range(CONV):
            start = 8 - (CONV - 1) + k
            term = taps[k : k + 1, :] * buf[start : start + LEN, :]
            total = term if total is None else total + term
        return silu(total)

    x = conv(buf_x, conv_x)
    bc = conv(buf_g, conv_g).astype(BF16)
    b, c = bc[:, :N], bc[:, N:]

    rows = lax.broadcasted_iota(jnp.int32, (LEN, LEN), 0)
    cols = lax.broadcasted_iota(jnp.int32, (LEN, LEN), 1)
    raw = own_v[:, WIDTH:] + got_v[:, WIDTH:] + bias[...]
    step = jnp.maximum(raw, 0.0) + jnp.log1p(jnp.exp(-jnp.abs(raw)))
    step = jnp.where((rows < live_to) & (cols < HEADS), step, 0.0)
    lower = (rows >= cols).astype(F32)
    total = jnp.dot(lower, -rate[...] * step, precision=lax.Precision.HIGHEST, preferred_element_type=F32)
    step_t = step.T
    total_t = total.T
    end_t = total_t[:, LEN - 1 : LEN]
    grow_t = jnp.exp(total_t)
    rest_t = jnp.exp(end_t - total_t) * step_t
    end = jnp.exp(end_t)

    scores = lax.dot_general(b, c, NT, preferred_element_type=F32)
    scores = jnp.where(rows <= cols, scores, 0.0)
    x_t = x.T
    init_all = init[...].reshape(CH, N)
    carried = lax.dot_general(init_all.astype(BF16), c, NT, preferred_element_type=F32)
    parts, kept = [], []
    for h in range(HEADS):
        at = slice(h * P_SIZE, (h + 1) * P_SIZE)
        decay = jnp.exp(jnp.minimum(total_t[h : h + 1, :] - total[:, h : h + 1], 0.0))
        mixing = (decay * scores).astype(BF16)
        weighted = (x_t[at] * step_t[h : h + 1, :]).astype(BF16)
        inner = jnp.dot(weighted, mixing, preferred_element_type=F32)
        parts.append(inner + carried[at] * grow_t[h : h + 1, :])
        kept.append((x_t[at] * rest_t[h : h + 1, :]).astype(BF16))
    added = jnp.dot(jnp.concatenate(kept, axis=0), b, preferred_element_type=F32)
    for h in range(HEADS):
        final_ref[0, h] = init[0, h] * end[h : h + 1, :] + added[h * P_SIZE : (h + 1) * P_SIZE]
    y = jnp.concatenate(parts, axis=0).T
    y = y + skip[...] * x
    low = y[:, :HALF] * silu(jnp.where(first, zo_v, zr_v))
    high = y[:, HALF:] * silu(jnp.where(first, zr_v, zo_v))
    square = jnp.sum(low * low, axis=-1, keepdims=True) + jnp.sum(high * high, axis=-1, keepdims=True)
    scale = lax.rsqrt(square * (1.0 / CH) + 1e-05)
    low = (low * scale * gain[:, :HALF]).astype(BF16)
    high = (high * scale * gain[:, HALF:]).astype(BF16)
    for side in range(2):
        place = info[5 + 2 * pl.program_id(0) + side]
        at = pl.ds(pl.multiple_of(place * (LEN // 2), LEN // 2), LEN // 2)
        out_ref[at, :HALF] = low[side * LEN // 2 : (side + 1) * LEN // 2]
        out_ref[at, HALF:] = high[side * LEN // 2 : (side + 1) * LEN // 2]


def scan(info, own, got, tail_x, tail_g, conv_x, conv_g, init, rate, bias, skip, gain):
    rollouts = init.shape[0]

    def rows(i, _):
        return (i, 0)

    def whole(i, _):
        return (0, 0)

    return pl.pallas_call(
        scan_kernel,
        grid_spec=pltpu.PrefetchScalarGridSpec(
            num_scalar_prefetch=1,
            grid=(rollouts,),
            in_specs=[
                pl.BlockSpec((LEN, WIDTH + 128), rows),
                pl.BlockSpec((LEN, WIDTH + 128), rows),
                pl.BlockSpec((1, CONV - 1, CH), lambda i, _: (i, 0, 0)),
                pl.BlockSpec((1, CONV - 1, 2 * N), lambda i, _: (i, 0, 0)),
                pl.BlockSpec((CONV, CH), whole),
                pl.BlockSpec((CONV, 2 * N), whole),
                pl.BlockSpec((1, HEADS, P_SIZE, N), lambda i, _: (i, 0, 0, 0)),
                pl.BlockSpec((1, 128), whole),
                pl.BlockSpec((1, 128), whole),
                pl.BlockSpec((1, CH), whole),
                pl.BlockSpec((1, CH), whole),
            ],
            out_specs=[
                pl.BlockSpec((rollouts * LEN, CH), whole),
                pl.BlockSpec((1, HEADS, P_SIZE, N), lambda i, _: (i, 0, 0, 0)),
            ],
            scratch_shapes=[pltpu.VMEM((8 + LEN, CH), F32), pltpu.VMEM((8 + LEN, 2 * N), F32)],
        ),
        out_shape=[
            jax.ShapeDtypeStruct((rollouts * LEN, CH), BF16),
            jax.ShapeDtypeStruct(init.shape, F32),
        ],
        compiler_params=pltpu.CompilerParams(vmem_limit_bytes=FAST),
        cost_estimate=pl.CostEstimate(flops=2_000_000_000, bytes_accessed=14_000_000, transcendentals=4_000_000),
        name="scan",
    )(info, own, got, tail_x, tail_g, conv_x, conv_g, init, rate, bias, skip, gain)


def place_kernel(table, kept_ref, given_ref, out_ref):
    for side, ref in enumerate((kept_ref, given_ref)):
        for index in range(8):
            start = pl.multiple_of(table[8 * side + index] * N, N)
            out_ref[:, pl.ds(start, N)] = ref[:, index * N : (index + 1) * N]


def place(table, kept, given):
    rows, width = kept.shape
    return pl.pallas_call(
        place_kernel,
        grid_spec=pltpu.PrefetchScalarGridSpec(
            num_scalar_prefetch=1,
            grid=(1,),
            in_specs=[pl.BlockSpec((rows, width), lambda i, _: (0, 0))] * 2,
            out_specs=pl.BlockSpec((rows, 2 * width), lambda i, _: (0, 0)),
        ),
        out_shape=jax.ShapeDtypeStruct((rows, 2 * width), BF16),
        compiler_params=pltpu.CompilerParams(vmem_limit_bytes=4 * 1024 * 1024),
        name="place",
    )(table, kept, given)


def multiply_kernel(split, own_ref, oth_ref, *refs):
    pieces, (first_ref, second_ref, rows) = refs[:-3], refs[-3:]
    per = own_ref.shape[0] // 4
    for dz in range(4):
        for f, ref in enumerate((own_ref, oth_ref)):
            rows[(2 * dz + f) * per : (2 * dz + f + 1) * per, :] = ref[dz * per : (dz + 1) * per, :]
    width = pieces[0].shape[1]
    for at, ref in enumerate(pieces):
        out_ref, column = (first_ref, at * width) if at < split else (second_ref, (at - split) * width)
        total = jnp.dot(rows[...], ref[...], preferred_element_type=F32)
        out_ref[:, column : column + width] = total.astype(BF16)


def multiply(own, oth, first, second):
    rows, depth = own.shape
    columns = [len(pieces) * pieces[0].shape[1] for pieces in (first, second)]
    total = sum(columns)
    return pl.pallas_call(
        functools.partial(multiply_kernel, len(first)),
        out_shape=[jax.ShapeDtypeStruct((2 * rows, n), BF16) for n in columns],
        scratch_shapes=[pltpu.VMEM((2 * rows, depth), BF16)],
        compiler_params=pltpu.CompilerParams(vmem_limit_bytes=36 * 1024 * 1024),
        cost_estimate=pl.CostEstimate(
            flops=4 * rows * depth * total, bytes_accessed=4 * rows * depth + 2 * total * (depth + 2 * rows), transcendentals=0
        ),
        name="multiply",
    )(own, oth, *first, *second)


def add(*terms):
    return functools.reduce(jnp.add, [t.astype(F32) for t in terms]).astype(BF16)


def reduce_z(parts):
    far = parts(2)
    half = far.shape[1] // 2
    far_a = lax.ppermute(far[:, :half], "z", ring(4, 1))
    far_b = lax.ppermute(far[:, half:], "z", ring(4, -1))
    up, down = parts(1), parts(3)
    up = jnp.concatenate([add(up[:, :half], far_a), up[:, half:]], axis=1)
    down = jnp.concatenate([down[:, :half], add(down[:, half:], far_b)], axis=1)
    from_below = lax.ppermute(up, "z", ring(4, 1))
    from_above = lax.ppermute(down, "z", ring(4, -1))
    return add(parts(0), from_below, from_above)


def reduce_z_first(value):
    block = value.shape[0] // 4
    mine = reduce_z(lambda dz: value[dz * block : (dz + 1) * block])
    mine = mine.reshape(2, 2, block // 4, mine.shape[1])
    return add(mine[:, 0], swap(mine[:, 1], "yl"))


def reduce_yl_first(value):
    block = value.shape[0] // 16
    value = value.reshape(8, 2, block, value.shape[1])
    value = add(value[:, 0], swap(value[:, 1], "yl")).reshape(8 * block, value.shape[3])
    mine = reduce_z(lambda dz: value[dz * 2 * block : (dz + 1) * 2 * block])
    return mine.reshape(2, block, mine.shape[1])


def shards(
    hidden_in,
    w_gate,
    w_input,
    w_groups,
    w_step,
    w_out,
    conv_input,
    conv_groups,
    tail_input,
    tail_groups,
    init_state,
    a_rate,
    step_bias,
    skip_gain,
    norm_gain,
    offsets,
):
    yh, x, c = lax.axis_index("yh"), lax.axis_index("x"), lax.axis_index("c")
    yl, z = lax.axis_index("yl"), lax.axis_index("z")
    group = ("c", "yl", "z")
    blocks = deal(w_groups, w_input, w_gate, w_step)
    s_own = assemble(lax.all_to_all(blocks, group, 0, 0, tiled=True))
    hidden_oth = swap(hidden_in, "c")

    half = KB // 2
    w_r, w_l = right(w_out), left(w_out)
    w_ft, w_fb = right(w_r[:KB]), left(w_l[KB:])
    w_f = jnp.concatenate([w_ft, w_fb], axis=0)
    s_r, s_l, s_o = right(s_own, w_r, w_l), left(s_own, w_r, w_l), over(s_own, w_ft, w_fb)
    w_o = over(w_out, s_o, w_f)
    s_ft, s_fb = right(s_r[:half], s_l), left(s_l[half:], s_r)
    near = project_part(
        hidden_in,
        hidden_oth,
        [((0, 0), s_own), ((0, 1), s_l), ((0, 3), s_r), ((1, 0), s_o), ((0, 2), (s_ft, s_fb))],
        16,
    )
    s_or, s_ol = right(s_o, s_ft, s_fb, w_o), left(s_o, s_ft, s_fb, w_o)
    s_oft, s_ofb = over(s_ft), over(s_fb)
    own, oth = project_part(
        hidden_in, hidden_oth, [((1, 1), s_ol), ((1, 3), s_or), ((1, 2), (s_oft, s_ofb))], 16, near
    )
    w_or, w_ol, w_of = right(w_o, s_or, s_ol), left(w_o, s_or, s_ol), over(w_f, s_oft, s_ofb)
    got = swap(oth, "c")

    def lanes(vector):
        return jnp.pad(vector, (0, 128 - HEADS))[None, :]

    at = jnp.arange(8)
    places = ((at % 4 - z) % 4) * 2 + (at // 4 + yl) % 2
    normed, final_state = scan(
        jnp.concatenate([jnp.reshape(c, (1,)), offsets, places]).astype(jnp.int32),
        own,
        got,
        tail_input,
        tail_groups,
        conv_input,
        conv_groups,
        init_state,
        lanes(a_rate),
        lanes(step_bias),
        jnp.repeat(skip_gain, P_SIZE)[None, :],
        norm_gain[None, :],
    )
    normed_oth = swap(after(normed, w_or, w_ol, w_of), "c")

    first, second = multiply(normed, normed_oth, [w_out, w_l, w_r, w_o], [w_f, w_ol, w_of, w_or])
    first, second = reduce_yl_first(first), reduce_z_first(second)
    sums = jnp.concatenate([first, second], axis=2)
    kept = sums[0]
    given = swap(sums[1], "c")

    order = [((yh + dy) % 2) * 4 + (x + dx) % 4 for dy, dx in ((0, 0), (0, 1), (0, 3), (1, 0), (0, 2), (1, 1), (1, 2), (1, 3))]
    mixed = place(jnp.stack([2 * p + core for core in (c, 1 - c) for p in order]).astype(jnp.int32), kept, given)
    return mixed, final_state


def solution(mesh):
    fine = Mesh(mesh.devices.reshape(2, 4, 2, 2, 4), ("yh", "x", "c", "yl", "z"))
    fsdp = ("yh", "x", "c")
    tp = ("yl", "z")
    return jax.shard_map(
        shards,
        mesh=fine,
        in_specs=(
            P(fsdp, None),
            P(fsdp + tp, None),
            P(fsdp + tp, None),
            P(fsdp + tp, None),
            P(fsdp + tp, None),
            P(tp, fsdp),
            P(None, tp),
            P(None, tp),
            P(fsdp, None, tp),
            P(fsdp, None, tp),
            P(fsdp, tp, None, None),
            P(tp),
            P(tp),
            P(tp),
            P(tp),
            P(fsdp),
        ),
        out_specs=(P(fsdp + tp, None), P(fsdp, tp, None, None)),
        check_vma=False,
    )
```

```python
import functools

import jax
import jax.numpy as jnp
from jax import lax
from jax.experimental import pallas as pl
from jax.experimental.pallas import tpu as pltpu
from jax.sharding import Mesh
from jax.sharding import PartitionSpec as P

P_SIZE = 64
N = 256
CONV = 4
LEN = 128
HEADS = 16
CH = HEADS * P_SIZE
HALF = CH // 2
WIDTH = 2 * N // 2 + CH
KB = 512
FAST = 48 * 1024 * 1024

F32 = jnp.float32
BF16 = jnp.bfloat16
NT = (((1,), (1,)), ((), ()))


def ring(n, step):
    return [(i, (i + step) % n) for i in range(n)]


def swap(value, axis):
    return lax.ppermute(value, axis, [(0, 1), (1, 0)])


def after(value, *others):
    return lax.optimization_barrier((value,) + others)[0]


def right(value, *others):
    return lax.ppermute(after(value, *others), "x", ring(4, 1))


def left(value, *others):
    return lax.ppermute(after(value, *others), "x", ring(4, -1))


def over(value, *others):
    return swap(after(value, *others), "yh")


def deal_kernel(groups_ref, input_ref, gate_ref, step_ref, out_ref):
    rows = groups_ref.shape[0]
    lanes = lax.broadcasted_iota(jnp.int32, (rows, 128), 1)
    steps = step_ref[...].astype(F32)
    for core in range(2):
        for t in range(8):
            here = slice((8 * core + t) * rows, (8 * core + t + 1) * rows)
            column = 0
            for ref in (groups_ref, input_ref, gate_ref):
                width = ref.shape[1] // 16
                first = (2 * t + core) * width
                out_ref[here, column : column + width] = ref[:, first : first + width]
                column += width
            turned = pltpu.roll(steps, (128 - HEADS * t) % 128, 1) if t else steps
            mine = (lanes >= 8 * core) & (lanes < 8 * core + 8)
            out_ref[here, column:] = jnp.where(mine, turned, 0.0).astype(BF16)


def deal(groups, inputs, gates, steps):
    return pl.pallas_call(
        deal_kernel,
        out_shape=jax.ShapeDtypeStruct((16 * groups.shape[0], WIDTH + 128), BF16),
        compiler_params=pltpu.CompilerParams(vmem_limit_bytes=60 * 1024 * 1024),
        name="deal",
    )(groups, inputs, gates, steps)


def assemble_kernel(blocks_ref, out_ref):
    out_ref[:KB, :] = blocks_ref[:, :WIDTH]
    out_ref[KB:, :] = jnp.zeros((16, WIDTH), BF16)
    steps = blocks_ref[:, WIDTH:].astype(F32).T
    out_ref[KB:, :KB] = steps[:16].astype(BF16)


def assemble(blocks):
    return pl.pallas_call(
        assemble_kernel,
        out_shape=jax.ShapeDtypeStruct((KB + 16, WIDTH), BF16),
        compiler_params=pltpu.CompilerParams(vmem_limit_bytes=16 * 1024 * 1024),
        name="assemble",
    )(blocks)


def project_kernel(steps, counts, last, table, own_hbm, oth_hbm, *refs):
    pieces, refs = list(refs[: sum(counts)]), refs[sum(counts) :]
    parts = [[pieces.pop(0) for _ in range(count)] for count in counts]
    final = len(parts) - 1
    sums, refs = (refs[:2], refs[2:]) if last else ((), refs)
    outs, (hid, weights, totals, results, sems) = refs[:2], refs[2:]
    rows = own_hbm.shape[0]
    width = weights.shape[2]
    half = KB // 2
    fetches = []
    for at, part in enumerate(parts):
        start = pl.multiple_of(table[at] * KB, KB)
        copies = [
            pltpu.make_async_copy(src.at[:, pl.ds(start, KB)], hid.at[at, which], sems.at[at, which])
            for which, src in enumerate((own_hbm, oth_hbm))
        ]
        for which, src in enumerate(part):
            into = weights.at[at, pl.ds(which * half, src.shape[0])]
            copies.append(pltpu.make_async_copy(src, into, sems.at[at, 2 + which]))
        fetches.append(copies)
        for copy in copies:
            copy.start()
    if last:
        fetches.append([pltpu.make_async_copy(src, totals.at[1, which], sems.at[len(parts), which]) for which, src in enumerate(sums)])
        for copy in fetches[-1]:
            copy.start()
    tile = 256
    stores = []
    for at in range(len(parts)):
        for copy in fetches[at]:
            copy.wait()
        if last and at == final:
            for copy in fetches[-1]:
                copy.wait()
        for which in (1, 0):
            for first in range(0, rows, tile):
                here = pl.ds(first, tile)
                block = hid[at, which, here]
                main = jnp.dot(block, weights[at, :KB], preferred_element_type=F32)
                extra = lax.dot_general(block, weights[at, KB:, :KB], NT, preferred_element_type=F32)
                extra = jnp.concatenate([extra, jnp.zeros((tile, 128 - steps), F32)], axis=1)
                if at:
                    main += totals[0, which, here, :width]
                    extra += totals[0, which, here, width:]
                if at < final:
                    totals[0, which, here, :width] = main
                    totals[0, which, here, width:] = extra
                else:
                    if last:
                        main += totals[1, which, here, :width]
                        extra += totals[1, which, here, width:]
                    results[which, here, :width] = main.astype(results.dtype)
                    results[which, here, width:] = extra.astype(results.dtype)
            if at == final:
                stores.append(pltpu.make_async_copy(results.at[which], outs[which], sems.at[len(parts) + 1, which]))
                stores[-1].start()
    for store in stores:
        store.wait()


def project_part(own, oth, pieces, steps, sums=()):
    rows, depth = own.shape
    x, yh = lax.axis_index("x"), lax.axis_index("yh")
    table = jnp.stack([4 * ((yh + dy) % 2) + (x + dx) % 4 for (dy, dx), _ in pieces]).astype(jnp.int32)
    pieces = [piece if isinstance(piece, tuple) else (piece,) for _, piece in pieces]
    counts = [len(piece) for piece in pieces]
    pieces = [part for piece in pieces for part in piece]
    width = pieces[0].shape[1]
    out_width = width + 128
    dtype = BF16 if sums else F32
    return pl.pallas_call(
        functools.partial(project_kernel, steps, counts, bool(sums)),
        grid_spec=pltpu.PrefetchScalarGridSpec(
            num_scalar_prefetch=1,
            grid=(1,),
            in_specs=[pl.BlockSpec(memory_space=pl.ANY)] * (2 + len(pieces) + len(sums)),
            out_specs=[pl.BlockSpec(memory_space=pl.ANY)] * 2,
            scratch_shapes=[
                pltpu.VMEM((len(counts), 2, rows, KB), BF16),
                pltpu.VMEM((len(counts), KB + 16, width), BF16),
                pltpu.VMEM((2 if sums else 1, 2, rows, out_width), F32),
                pltpu.VMEM((2, rows, out_width), dtype),
                pltpu.SemaphoreType.DMA((len(counts) + 2, 4)),
            ],
        ),
        out_shape=[jax.ShapeDtypeStruct((rows, out_width), dtype)] * 2,
        compiler_params=pltpu.CompilerParams(vmem_limit_bytes=FAST),
        cost_estimate=pl.CostEstimate(
            flops=4 * rows * KB * width * len(counts),
            bytes_accessed=2 * KB * (2 * rows + width) * len(counts) + 12 * rows * width,
            transcendentals=0,
        ),
        name="project",
    )(table, own, oth, *pieces, *sums)


def silu(v):
    return v / (1.0 + jnp.exp(-v))


def scan_kernel(
    info, own, got, tail_x, tail_g, conv_x, conv_g, init, rate, bias, skip, gain, out_ref, final_ref, buf_x, buf_g
):
    first = info[0] == 0
    live_to = info[1 + pl.program_id(0)]

    buf_x[8 - (CONV - 1) : 8, :] = tail_x[0].astype(F32)
    buf_g[8 - (CONV - 1) : 8, :] = tail_g[0].astype(F32)
    own_v, got_v = own[...].astype(F32), got[...].astype(F32)
    bo_v, br_v = own_v[:, :N], got_v[:, :N]
    xo_v, xr_v = own_v[:, N : N + HALF], got_v[:, N : N + HALF]
    zo_v, zr_v = own_v[:, N + HALF : WIDTH], got_v[:, N + HALF : WIDTH]
    buf_x[8:, :HALF] = jnp.where(first, xo_v, xr_v)
    buf_x[8:, HALF:] = jnp.where(first, xr_v, xo_v)
    buf_g[8:, :N] = jnp.where(first, bo_v, br_v)
    buf_g[8:, N:] = jnp.where(first, br_v, bo_v)

    def conv(buf, taps_ref):
        taps = taps_ref[...].astype(F32)
        total = None
        for k in range(CONV):
            start = 8 - (CONV - 1) + k
            term = taps[k : k + 1, :] * buf[start : start + LEN, :]
            total = term if total is None else total + term
        return silu(total)

    x = conv(buf_x, conv_x)
    bc = conv(buf_g, conv_g).astype(BF16)
    b, c = bc[:, :N], bc[:, N:]

    rows = lax.broadcasted_iota(jnp.int32, (LEN, LEN), 0)
    cols = lax.broadcasted_iota(jnp.int32, (LEN, LEN), 1)
    raw = own_v[:, WIDTH:] + got_v[:, WIDTH:] + bias[...]
    step = jnp.maximum(raw, 0.0) + jnp.log1p(jnp.exp(-jnp.abs(raw)))
    step = jnp.where((rows < live_to) & (cols < HEADS), step, 0.0)
    lower = (rows >= cols).astype(F32).astype(BF16)
    left_over = -rate[...] * step
    pieces = []
    for _ in range(3):
        pieces.append(left_over.astype(BF16))
        left_over = left_over - pieces[-1].astype(F32)
    total = jnp.dot(
        jnp.concatenate([lower] * 3, axis=1), jnp.concatenate(pieces, axis=0), preferred_element_type=F32
    )
    step_t = step.T
    total_t = total.T
    end_t = total_t[:, LEN - 1 : LEN]
    grow_t = jnp.exp(total_t)
    rest_t = jnp.exp(end_t - total_t) * step_t
    end = jnp.exp(end_t)

    scores = lax.dot_general(b, c, NT, preferred_element_type=F32)
    scores = jnp.where(rows <= cols, scores, 0.0)
    x_t = x.T
    init_all = init[...].reshape(CH, N)
    carried = lax.dot_general(init_all.astype(BF16), c, NT, preferred_element_type=F32)
    parts, kept = [], []
    for h in range(HEADS):
        at = slice(h * P_SIZE, (h + 1) * P_SIZE)
        decay = jnp.exp(jnp.minimum(total_t[h : h + 1, :] - total[:, h : h + 1], 0.0))
        mixing = (decay * scores).astype(BF16)
        weighted = (x_t[at] * step_t[h : h + 1, :]).astype(BF16)
        inner = jnp.dot(weighted, mixing, preferred_element_type=F32)
        parts.append(inner + carried[at] * grow_t[h : h + 1, :])
        kept.append((x_t[at] * rest_t[h : h + 1, :]).astype(BF16))
    added = jnp.dot(jnp.concatenate(kept, axis=0), b, preferred_element_type=F32)
    for h in range(HEADS):
        final_ref[0, h] = init[0, h] * end[h : h + 1, :] + added[h * P_SIZE : (h + 1) * P_SIZE]
    y = jnp.concatenate(parts, axis=0).T
    y = y + skip[...] * x
    low = y[:, :HALF] * silu(jnp.where(first, zo_v, zr_v))
    high = y[:, HALF:] * silu(jnp.where(first, zr_v, zo_v))
    square = jnp.sum(low * low, axis=-1, keepdims=True) + jnp.sum(high * high, axis=-1, keepdims=True)
    scale = lax.rsqrt(square * (1.0 / CH) + 1e-05)
    low = (low * scale * gain[:, :HALF]).astype(BF16)
    high = (high * scale * gain[:, HALF:]).astype(BF16)
    for side in range(2):
        place = info[5 + 2 * pl.program_id(0) + side]
        at = pl.ds(pl.multiple_of(place * (LEN // 2), LEN // 2), LEN // 2)
        out_ref[at, :HALF] = low[side * LEN // 2 : (side + 1) * LEN // 2]
        out_ref[at, HALF:] = high[side * LEN // 2 : (side + 1) * LEN // 2]


def scan(info, own, got, tail_x, tail_g, conv_x, conv_g, init, rate, bias, skip, gain):
    rollouts = init.shape[0]

    def rows(i, _):
        return (i, 0)

    def whole(i, _):
        return (0, 0)

    return pl.pallas_call(
        scan_kernel,
        grid_spec=pltpu.PrefetchScalarGridSpec(
            num_scalar_prefetch=1,
            grid=(rollouts,),
            in_specs=[
                pl.BlockSpec((LEN, WIDTH + 128), rows),
                pl.BlockSpec((LEN, WIDTH + 128), rows),
                pl.BlockSpec((1, CONV - 1, CH), lambda i, _: (i, 0, 0)),
                pl.BlockSpec((1, CONV - 1, 2 * N), lambda i, _: (i, 0, 0)),
                pl.BlockSpec((CONV, CH), whole),
                pl.BlockSpec((CONV, 2 * N), whole),
                pl.BlockSpec((1, HEADS, P_SIZE, N), lambda i, _: (i, 0, 0, 0)),
                pl.BlockSpec((1, 128), whole),
                pl.BlockSpec((1, 128), whole),
                pl.BlockSpec((1, CH), whole),
                pl.BlockSpec((1, CH), whole),
            ],
            out_specs=[
                pl.BlockSpec((rollouts * LEN, CH), whole),
                pl.BlockSpec((1, HEADS, P_SIZE, N), lambda i, _: (i, 0, 0, 0)),
            ],
            scratch_shapes=[pltpu.VMEM((8 + LEN, CH), F32), pltpu.VMEM((8 + LEN, 2 * N), F32)],
        ),
        out_shape=[
            jax.ShapeDtypeStruct((rollouts * LEN, CH), BF16),
            jax.ShapeDtypeStruct(init.shape, F32),
        ],
        compiler_params=pltpu.CompilerParams(vmem_limit_bytes=FAST),
        cost_estimate=pl.CostEstimate(flops=2_000_000_000, bytes_accessed=14_000_000, transcendentals=4_000_000),
        name="scan",
    )(info, own, got, tail_x, tail_g, conv_x, conv_g, init, rate, bias, skip, gain)


def place_kernel(table, kept_ref, given_ref, out_ref):
    for side, ref in enumerate((kept_ref, given_ref)):
        for index in range(8):
            start = pl.multiple_of(table[8 * side + index] * N, N)
            out_ref[:, pl.ds(start, N)] = ref[:, index * N : (index + 1) * N]


def place(table, kept, given):
    rows, width = kept.shape
    return pl.pallas_call(
        place_kernel,
        grid_spec=pltpu.PrefetchScalarGridSpec(
            num_scalar_prefetch=1,
            grid=(1,),
            in_specs=[pl.BlockSpec((rows, width), lambda i, _: (0, 0))] * 2,
            out_specs=pl.BlockSpec((rows, 2 * width), lambda i, _: (0, 0)),
        ),
        out_shape=jax.ShapeDtypeStruct((rows, 2 * width), BF16),
        compiler_params=pltpu.CompilerParams(vmem_limit_bytes=4 * 1024 * 1024),
        name="place",
    )(table, kept, given)


def multiply_kernel(split, own_ref, oth_ref, *refs):
    pieces, (first_ref, second_ref, rows) = refs[:-3], refs[-3:]
    per = own_ref.shape[0] // 4
    for dz in range(4):
        for f, ref in enumerate((own_ref, oth_ref)):
            rows[(2 * dz + f) * per : (2 * dz + f + 1) * per, :] = ref[dz * per : (dz + 1) * per, :]
    width = pieces[0].shape[1]
    for at, ref in enumerate(pieces):
        out_ref, column = (first_ref, at * width) if at < split else (second_ref, (at - split) * width)
        total = jnp.dot(rows[...], ref[...], preferred_element_type=F32)
        out_ref[:, column : column + width] = total.astype(BF16)


def multiply(own, oth, first, second):
    rows, depth = own.shape
    columns = [len(pieces) * pieces[0].shape[1] for pieces in (first, second)]
    total = sum(columns)
    return pl.pallas_call(
        functools.partial(multiply_kernel, len(first)),
        out_shape=[jax.ShapeDtypeStruct((2 * rows, n), BF16) for n in columns],
        scratch_shapes=[pltpu.VMEM((2 * rows, depth), BF16)],
        compiler_params=pltpu.CompilerParams(vmem_limit_bytes=36 * 1024 * 1024),
        cost_estimate=pl.CostEstimate(
            flops=4 * rows * depth * total, bytes_accessed=4 * rows * depth + 2 * total * (depth + 2 * rows), transcendentals=0
        ),
        name="multiply",
    )(own, oth, *first, *second)


def add(*terms):
    return functools.reduce(jnp.add, [t.astype(F32) for t in terms]).astype(BF16)


def reduce_z(parts):
    far = parts(2)
    half = far.shape[1] // 2
    far_a = lax.ppermute(far[:, :half], "z", ring(4, 1))
    far_b = lax.ppermute(far[:, half:], "z", ring(4, -1))
    up, down = parts(1), parts(3)
    up = jnp.concatenate([add(up[:, :half], far_a), up[:, half:]], axis=1)
    down = jnp.concatenate([down[:, :half], add(down[:, half:], far_b)], axis=1)
    from_below = lax.ppermute(up, "z", ring(4, 1))
    from_above = lax.ppermute(down, "z", ring(4, -1))
    return add(parts(0), from_below, from_above)


def reduce_z_first(value):
    block = value.shape[0] // 4
    mine = reduce_z(lambda dz: value[dz * block : (dz + 1) * block])
    mine = mine.reshape(2, 2, block // 4, mine.shape[1])
    return add(mine[:, 0], swap(mine[:, 1], "yl"))


def reduce_yl_first(value):
    block = value.shape[0] // 16
    value = value.reshape(8, 2, block, value.shape[1])
    value = add(value[:, 0], swap(value[:, 1], "yl")).reshape(8 * block, value.shape[3])
    mine = reduce_z(lambda dz: value[dz * 2 * block : (dz + 1) * 2 * block])
    return mine.reshape(2, block, mine.shape[1])


def shards(
    hidden_in,
    w_gate,
    w_input,
    w_groups,
    w_step,
    w_out,
    conv_input,
    conv_groups,
    tail_input,
    tail_groups,
    init_state,
    a_rate,
    step_bias,
    skip_gain,
    norm_gain,
    offsets,
):
    yh, x, c = lax.axis_index("yh"), lax.axis_index("x"), lax.axis_index("c")
    yl, z = lax.axis_index("yl"), lax.axis_index("z")
    group = ("c", "yl", "z")
    blocks = deal(w_groups, w_input, w_gate, w_step)
    s_own = assemble(lax.all_to_all(blocks, group, 0, 0, tiled=True))
    hidden_oth = swap(hidden_in, "c")

    half = KB // 2
    w_r, w_l = right(w_out), left(w_out)
    w_ft, w_fb = right(w_r[:KB]), left(w_l[KB:])
    w_f = jnp.concatenate([w_ft, w_fb], axis=0)
    s_r, s_l, s_o = right(s_own, w_r, w_l), left(s_own, w_r, w_l), over(s_own, w_ft, w_fb)
    w_o = over(w_out, s_o, w_f)
    s_ft, s_fb = right(s_r[:half], s_l), left(s_l[half:], s_r)
    near = project_part(
        hidden_in,
        hidden_oth,
        [((0, 0), s_own), ((0, 1), s_l), ((0, 3), s_r), ((1, 0), s_o), ((0, 2), (s_ft, s_fb))],
        16,
    )
    s_or, s_ol = right(s_o, s_ft, s_fb, w_o), left(s_o, s_ft, s_fb, w_o)
    s_oft, s_ofb = over(s_ft), over(s_fb)
    own, oth = project_part(
        hidden_in, hidden_oth, [((1, 1), s_ol), ((1, 3), s_or), ((1, 2), (s_oft, s_ofb))], 16, near
    )
    w_or, w_ol, w_of = right(w_o, s_or, s_ol), left(w_o, s_or, s_ol), over(w_f, s_oft, s_ofb)
    got = swap(oth, "c")

    def lanes(vector):
        return jnp.pad(vector, (0, 128 - HEADS))[None, :]

    at = jnp.arange(8)
    places = ((at % 4 - z) % 4) * 2 + (at // 4 + yl) % 2
    normed, final_state = scan(
        jnp.concatenate([jnp.reshape(c, (1,)), offsets, places]).astype(jnp.int32),
        own,
        got,
        tail_input,
        tail_groups,
        conv_input,
        conv_groups,
        init_state,
        lanes(a_rate),
        lanes(step_bias),
        jnp.repeat(skip_gain, P_SIZE)[None, :],
        norm_gain[None, :],
    )
    normed_oth = swap(after(normed, w_or, w_ol, w_of), "c")

    first, second = multiply(normed, normed_oth, [w_out, w_l, w_r, w_o], [w_f, w_ol, w_of, w_or])
    first, second = reduce_yl_first(first), reduce_z_first(second)
    sums = jnp.concatenate([first, second], axis=2)
    kept = sums[0]
    given = swap(sums[1], "c")

    order = [((yh + dy) % 2) * 4 + (x + dx) % 4 for dy, dx in ((0, 0), (0, 1), (0, 3), (1, 0), (0, 2), (1, 1), (1, 2), (1, 3))]
    mixed = place(jnp.stack([2 * p + core for core in (c, 1 - c) for p in order]).astype(jnp.int32), kept, given)
    return mixed, final_state


def solution(mesh):
    fine = Mesh(mesh.devices.reshape(2, 4, 2, 2, 4), ("yh", "x", "c", "yl", "z"))
    fsdp = ("yh", "x", "c")
    tp = ("yl", "z")
    return jax.shard_map(
        shards,
        mesh=fine,
        in_specs=(
            P(fsdp, None),
            P(fsdp + tp, None),
            P(fsdp + tp, None),
            P(fsdp + tp, None),
            P(fsdp + tp, None),
            P(tp, fsdp),
            P(None, tp),
            P(None, tp),
            P(fsdp, None, tp),
            P(fsdp, None, tp),
            P(fsdp, tp, None, None),
            P(tp),
            P(tp),
            P(tp),
            P(tp),
            P(fsdp),
        ),
        out_specs=(P(fsdp + tp, None), P(fsdp, tp, None, None)),
        check_vma=False,
    )
```
